32 devices in a mesh: row: 4 (over x, core), col: 8 (over z, y).
Axes of the slice: x: 2, y: 2, z: 4, core: 2. Of those that a mesh axis runs over, the one named last changes fastest.
Arguments:
- blocks: bfloat16 [1536, 27, 48, 48], P(('row', 'col')), may hold values from -0.59765625 to 0.59765625
- prolong: bfloat16 [1536, 48, 48], P(('row', 'col')), may hold values from -0.875 to 0.875
- columns: int32 [1536, 27], P(('row', 'col')), may hold values from 0 to 191
- aggregate: int32 [1536], P(('row', 'col')), may hold values from 0 to 15
- slots: int32 [1536, 27], P(('row', 'col')), may hold values from 0 to 26
Outputs:
- coarse: float32 [64, 27, 2304], P('row', None, 'col')
The draws below stay inside these ranges and needn't reach their ends.
Inputs may be any that keep to these rules, and one draw needn't show every extreme that they name: `columns`: a fine block row's neighbours all lie in its column tile: the fine block rows of the devices with the same col index, in order of their row index.
All inputs are finite; a program needn't handle non-finite values.
Results may differ from the reference program's by a relative error of at most 0.0029.
Values may be sent and summed in bfloat16 or wider, within the bound.
A program may use at most 192 MiB of HBM per device.

```python
import jax
import jax.numpy as jnp
from jax import lax

B = 48
K = 27
KC = 27
ROWS_DEV = 48
CR_SLAB = 16
NB = 1536
N_ROW = 4
N_COL = 8


def set_ends(result, key, least, high):
    extent = result.shape
    index_at = [jax.random.randint(jax.random.fold_in(key, axis), (), 0, extent[axis]) for axis in range(len(extent))]
    result = result.at[tuple(index_at)].set(least)
    longest = extent.index(max(extent))
    index_at[longest] = (index_at[longest] + 1) % extent[longest]
    return result.at[tuple(index_at)].set(high)


def levels(own_key, dims, shards, low, largest):
    gain = 1.0
    for axis_at, blocks in shards:
        steps = jax.random.uniform(jax.random.fold_in(jax.random.fold_in(own_key, 6), axis_at), (blocks,), jnp.float32, low / len(shards), largest / len(shards))
        gain = gain * jnp.repeat(jnp.exp(steps), dims[axis_at] // blocks).reshape((-1,) + (1,) * (len(dims) - 1 - axis_at))
    return gain


def normal_values(rng, dims, scale, most, shards=(), kind=jnp.bfloat16):
    level = levels(rng, dims, shards, -0.22, 0.18) if shards else 1.0
    result = jax.random.normal(rng, dims, jnp.float32) * scale * level
    return jnp.minimum(jnp.maximum(result, -most), most).astype(kind)


def setup_inputs(seed: int = 0) -> dict:
    keys = jax.random.split(jax.random.key(seed), 6)
    return {
        "blocks": normal_values(keys[0], (NB, K, B, B), 0.1, 0.59765625, ((0, 32),)),
        "prolong": normal_values(keys[1], (NB, B, B), B ** -0.5, 0.875, ((0, 32),)),
        "columns": set_ends(jax.random.randint(keys[2], (NB, K), 0, ROWS_DEV * N_ROW), jax.random.fold_in(keys[2], 1), 0, (ROWS_DEV * N_ROW) - 1).astype(jnp.int32),
        "aggregate": set_ends(jax.random.randint(keys[3], (NB,), 0, CR_SLAB), jax.random.fold_in(keys[3], 1), 0, CR_SLAB - 1).astype(jnp.int32),
        "slots": set_ends(jax.random.randint(keys[4], (NB, K), 0, KC), jax.random.fold_in(keys[4], 1), 0, KC - 1).astype(jnp.int32),
    }


def reference(blocks, prolong, columns, aggregate, slots):
    owners_all = N_ROW * N_COL
    block_parts = blocks.reshape(owners_all, ROWS_DEV, K, B, B)
    prolong_parts = prolong.reshape(owners_all, ROWS_DEV, B, B)
    column_parts = columns.reshape(owners_all, ROWS_DEV, K)
    aggregate_parts = aggregate.reshape(owners_all, ROWS_DEV)
    slot_parts = slots.reshape(owners_all, ROWS_DEV, K)

    def accumulate(total, item):
        owner, local_blocks, local_prolong, local_columns, local_aggregate, local_slots = item
        slab_index = owner // N_COL
        tile_index = owner % N_COL
        neighbour = (local_columns // ROWS_DEV) * (N_COL * ROWS_DEV) + tile_index * ROWS_DEV + local_columns % ROWS_DEV
        picked = jnp.take(prolong, neighbour.astype(jnp.int32), axis=0)
        product = jnp.einsum("rkab,rkbc->rkac", local_blocks.astype(jnp.float32), picked.astype(jnp.float32))
        product = lax.optimization_barrier(product.astype(jnp.bfloat16)).astype(jnp.float32)
        term = jnp.einsum("rba,rkbc->rkac", local_prolong.astype(jnp.float32), product)
        target = ((slab_index * CR_SLAB + local_aggregate)[:, None] * KC + local_slots).astype(jnp.int32)
        total = total.at[target.reshape(-1)].add(term.reshape(-1, B * B))
        return total, None

    owners = jnp.arange(owners_all, dtype=jnp.int32)
    start = jnp.zeros((N_ROW * CR_SLAB * KC, B * B), jnp.float32)
    total, _ = lax.scan(accumulate, start, (owners, block_parts, prolong_parts, column_parts, aggregate_parts, slot_parts))
    return total.reshape(N_ROW * CR_SLAB, KC, B * B)
```

```python
import functools

import jax
import jax.numpy as jnp
from jax import lax
from jax.experimental import pallas as pl
from jax.experimental.pallas import tpu as pltpu
from jax.sharding import PartitionSpec as P

KC = 27
CR_SLAB = 16
MESH = pl.DeviceIdType.MESH
LANES = 128
GROUPS = 4
GROUP = 112
ROWS_STEP = 4
HALVES = ((0, 64), (64, 48))


def placement(rows, source, dest):
    row = lax.broadcasted_iota(jnp.int32, (rows, LANES), 0)
    lane = lax.broadcasted_iota(jnp.int32, (rows, LANES), 1)
    keep = (row - source == lane - dest) & (row >= source) & (row < source + 48)
    return jnp.where(keep, 1.0, 0.0).astype(jnp.bfloat16)


def move(value, matrix):
    return jnp.dot(value, matrix, preferred_element_type=jnp.float32).astype(jnp.bfloat16)


def gather_kernel(p_ref, out_ref, packed, send_sem, recv_sem):
    rows, width = p_ref.shape[0], p_ref.shape[1]
    half = rows // 2
    me = lax.axis_index("row")
    core, x = me % 2, me // 2
    other = x * 2 + 1 - core
    across = (1 - x) * 2 + core
    diagonal = (1 - x) * 2 + 1 - core

    barrier = pltpu.get_barrier_semaphore()
    for peer in (other, across):
        pl.semaphore_signal(barrier, inc=1, device_id={"row": peer}, device_id_type=MESH)

    low = p_ref[:half].reshape(half * width, width)
    high = p_ref[half:].reshape(half * width, width)
    first, second = placement(width, 0, 0), placement(width, 0, 48)
    both = jnp.dot(low, first, preferred_element_type=jnp.float32) + jnp.dot(
        high, second, preferred_element_type=jnp.float32
    )
    packed[0] = both.astype(jnp.bfloat16)
    pl.semaphore_wait(barrier, 2)

    def send(source, dest, peer):
        copy = pltpu.make_async_remote_copy(
            src_ref=packed.at[source],
            dst_ref=packed.at[dest],
            send_sem=send_sem.at[dest],
            recv_sem=recv_sem.at[dest],
            device_id={"row": peer},
            device_id_type=MESH,
        )
        copy.start()
        return copy

    def unpack(slot, owner):
        value = packed[slot]
        out_ref[pl.ds(owner * rows, half)] = move(value, placement(LANES, 0, 0)).reshape(half, width, LANES)
        out_ref[pl.ds(owner * rows + half, half)] = move(value, placement(LANES, 48, 0)).reshape(half, width, LANES)

    far = send(0, 2, across)
    near = send(0, 1, other)
    unpack(0, me)
    near.wait_recv()
    unpack(1, other)
    far.wait_recv()
    relay = send(2, 3, other)
    unpack(2, across)
    relay.wait_recv()
    unpack(3, diagonal)
    far.wait_send()
    near.wait_send()
    relay.wait_send()


def gather_rows(prolong, n_row):
    rows, width = prolong.shape[0], prolong.shape[1]
    return pl.pallas_call(
        gather_kernel,
        out_shape=jax.ShapeDtypeStruct((n_row * rows, width, LANES), jnp.bfloat16),
        in_specs=[pl.BlockSpec(memory_space=pltpu.VMEM)],
        out_specs=pl.BlockSpec(memory_space=pltpu.VMEM),
        scratch_shapes=[
            pltpu.VMEM((4, rows // 2 * width, LANES), jnp.bfloat16),
            pltpu.SemaphoreType.DMA((4,)),
            pltpu.SemaphoreType.DMA((4,)),
        ],
        compiler_params=pltpu.CompilerParams(
            collective_id=0, has_side_effects=True, vmem_limit_bytes=24 * 2**20
        ),
        name="gather_prolong",
    )(prolong)


def product_kernel(col_ref, slot_ref, agg_ref, tile_ref, own_ref, blk_ref, out_ref, acc):
    step = pl.program_id(0)
    width = own_ref.shape[1]
    neighbours = blk_ref.shape[1]

    @pl.when(step == 0)
    def _():
        @pl.loop(0, acc.shape[0] // 384)
        def _(at):
            acc[pl.ds(at * 384, 384), :] = jnp.zeros((384, LANES), jnp.float32)

    @pl.loop(0, ROWS_STEP)
    def _(r):
        i = step * ROWS_STEP + r
        turned = own_ref[i].astype(jnp.float32).T.astype(jnp.bfloat16)
        aggregate = agg_ref[i]
        for k in range(neighbours):
            product = jnp.dot(
                blk_ref[r, k], tile_ref[col_ref[i, k]], preferred_element_type=jnp.float32
            ).astype(jnp.bfloat16)
            term = jnp.dot(turned, product, preferred_element_type=jnp.float32)
            base = pl.multiple_of((slot_ref[i, k] * CR_SLAB + aggregate) * width, width)
            acc[pl.ds(base, width), :] += term

    @pl.when(step == pl.num_programs(0) - 1)
    def _():
        lane = lax.broadcasted_iota(jnp.int32, (16, LANES), 1)

        @pl.loop(0, 8 * (GROUP // 16))
        def _(at):
            d, s = at // (GROUP // 16), at % (GROUP // 16)
            sums = [None] * 9
            for q in range(GROUPS):
                for r in range(6):
                    start = (GROUP * q + 16 * s) * width + 6 * d + r
                    offset = (q * 6 + r) * 48
                    j, shift = offset // LANES, offset % LANES
                    value = acc[pl.ds(start, 16, stride=width), :]
                    if shift:
                        value = pltpu.roll(value, shift, 1)
                    over = shift + 48 - LANES
                    if over > 0:
                        spill = jnp.where(lane < over, value, 0.0)
                        value = jnp.where(lane < over, 0.0, value)
                        sums[j + 1] = spill
                    sums[j] = value if sums[j] is None else sums[j] + value
            for j in range(9):
                out_ref[d, pl.ds(pl.multiple_of(16 * s, 16), 16), j * LANES:(j + 1) * LANES] = sums[j].astype(jnp.bfloat16)


def products(tile, prolong, blocks, columns, aggregate, slots):
    rows, neighbours, width = blocks.shape[0], blocks.shape[1], blocks.shape[2]
    smem = pl.BlockSpec(memory_space=pltpu.SMEM)
    vmem = pl.BlockSpec(memory_space=pltpu.VMEM)
    flops = rows * neighbours * width**3 * 4
    return pl.pallas_call(
        product_kernel,
        grid=(rows // ROWS_STEP,),
        out_shape=jax.ShapeDtypeStruct((8, GROUP, 9 * LANES), jnp.bfloat16),
        in_specs=[
            smem,
            smem,
            smem,
            vmem,
            vmem,
            pl.BlockSpec((ROWS_STEP, neighbours, width, width), lambda g: (g, 0, 0, 0)),
        ],
        out_specs=vmem,
        scratch_shapes=[pltpu.VMEM((GROUPS * GROUP * width, LANES), jnp.float32)],
        compiler_params=pltpu.CompilerParams(vmem_limit_bytes=40 * 2**20),
        cost_estimate=pl.CostEstimate(flops=flops, bytes_accessed=20 * 2**20, transcendentals=0),
        name="triple_products",
    )(columns, slots, aggregate, tile, prolong, blocks)


def scatter_kernel(x_ref, out_ref, ybuf, zsend, zbuf, own, ysend_sem, yrecv_sem, zsend_sem, zrecv_sem):
    me = lax.axis_index("col")
    y, z = me % 2, me // 2
    partner = z * 2 + 1 - y
    offsets = (2, 1, 3, 0)
    targets = [(z + offset) % 4 for offset in offsets]

    barrier = pltpu.get_barrier_semaphore()
    for peer in [partner] + [t * 2 + y for t in targets[:3]]:
        pl.semaphore_signal(barrier, inc=1, device_id={"col": peer}, device_id_type=MESH)
    pl.semaphore_wait(barrier, 4)

    ycopies, zcopies = {}, {}
    for s in range(4):
        for h, (begin, size) in enumerate(HALVES):
            copy = pltpu.make_async_remote_copy(
                src_ref=x_ref.at[targets[s] * 2 + 1 - y, pl.ds(begin, size)],
                dst_ref=ybuf.at[s, pl.ds(begin, size)],
                send_sem=ysend_sem.at[s, h],
                recv_sem=yrecv_sem.at[s, h],
                device_id={"col": partner},
                device_id_type=MESH,
            )
            copy.start()
            ycopies[s, h] = copy

    for s in range(4):
        for h, (begin, size) in enumerate(HALVES):
            ycopies[s, h].wait_recv()

            @pl.loop(begin // 16, (begin + size) // 16)
            def _(at):
                rows = pl.ds(pl.multiple_of(at * 16, 16), 16)
                total = x_ref[targets[s] * 2 + y, rows, :].astype(jnp.float32) + ybuf[s, rows, :].astype(jnp.float32)
                if s < 3:
                    zsend[s, rows, :] = total.astype(jnp.bfloat16)
                else:
                    own[rows, :] = total

            if s < 3:
                copy = pltpu.make_async_remote_copy(
                    src_ref=zsend.at[s, pl.ds(begin, size)],
                    dst_ref=zbuf.at[s, pl.ds(begin, size)],
                    send_sem=zsend_sem.at[s, h],
                    recv_sem=zrecv_sem.at[s, h],
                    device_id={"col": targets[s] * 2 + y},
                    device_id_type=MESH,
                )
                copy.start()
                zcopies[s, h] = copy

    for copy in zcopies.values():
        copy.wait_recv()

    lane = lax.broadcasted_iota(jnp.int32, (16, LANES), 1)

    def unpack(at, groups):
        rows = pl.ds(pl.multiple_of(at * 16, 16), 16)
        total = own[rows, :]
        for s in range(3):
            total = total + zbuf[s, rows, :].astype(jnp.float32)
        for q in range(groups):
            j, shift = 288 * q // LANES, 288 * q % LANES
            turned = [total[:, (j + m) * LANES:(j + m + 1) * LANES] for m in range(3)]
            if shift:
                turned = [pltpu.roll(piece, LANES - shift, 1) for piece in turned]
            target = pl.ds(pl.multiple_of(GROUP * q + at * 16, 16), 16)
            for m in range(2):
                piece = turned[m]
                if shift:
                    piece = jnp.where(lane < LANES - shift, piece, turned[m + 1])
                out_ref[target, m * LANES:(m + 1) * LANES] = piece
            out_ref[target, 256:288] = turned[2][:, :32]

    @pl.loop(0, 6)
    def _(at):
        unpack(at, 4)

    unpack(6, 3)

    for copy in list(ycopies.values()) + list(zcopies.values()):
        copy.wait_send()


def scatter_cols(packed):
    half = len(HALVES)
    return pl.pallas_call(
        scatter_kernel,
        out_shape=jax.ShapeDtypeStruct((KC * CR_SLAB, 288), jnp.float32),
        in_specs=[pl.BlockSpec(memory_space=pltpu.VMEM)],
        out_specs=pl.BlockSpec(memory_space=pltpu.VMEM),
        scratch_shapes=[
            pltpu.VMEM((4, GROUP, 9 * LANES), jnp.bfloat16),
            pltpu.VMEM((3, GROUP, 9 * LANES), jnp.bfloat16),
            pltpu.VMEM((3, GROUP, 9 * LANES), jnp.bfloat16),
            pltpu.VMEM((GROUP, 9 * LANES), jnp.float32),
            pltpu.SemaphoreType.DMA((4, half)),
            pltpu.SemaphoreType.DMA((4, half)),
            pltpu.SemaphoreType.DMA((3, half)),
            pltpu.SemaphoreType.DMA((3, half)),
        ],
        compiler_params=pltpu.CompilerParams(
            collective_id=1, has_side_effects=True, vmem_limit_bytes=24 * 2**20
        ),
        name="scatter_cols",
    )(packed)


def shards(n_row, blocks, prolong, columns, aggregate, slots):
    tile = gather_rows(prolong, n_row)
    packed = products(tile, prolong, blocks, columns, aggregate, slots)
    result = scatter_cols(packed)
    return result.reshape(KC, CR_SLAB, 288).transpose(1, 0, 2)


def shards_any(blocks, prolong, columns, aggregate, slots):
    width = blocks.shape[2]
    tile = lax.all_gather(prolong, "row", axis=0, tiled=True)
    picked = jnp.take(tile, columns, axis=0)
    product = jnp.einsum(
        "rkab,rkbc->rkac", blocks, picked, preferred_element_type=jnp.float32
    ).astype(jnp.bfloat16)
    term = jnp.einsum("rba,rkbc->rkac", prolong, product, preferred_element_type=jnp.float32)
    target = (aggregate[:, None] * KC + slots).reshape(-1)
    partial_value = jax.ops.segment_sum(
        term.reshape(-1, width * width), target, num_segments=CR_SLAB * KC
    )
    partial_value = partial_value.reshape(CR_SLAB, KC, width * width)
    summed = lax.psum(partial_value, "col")
    share = width * width // lax.axis_size("col")
    return lax.dynamic_slice_in_dim(summed, lax.axis_index("col") * share, share, 2)


def solution(mesh):
    n_row, n_col = mesh.shape["row"], mesh.shape["col"]
    body = functools.partial(shards, n_row) if (n_row, n_col) == (4, 8) else shards_any
    return jax.shard_map(
        body,
        mesh=mesh,
        in_specs=(
            P(("row", "col"), None, None, None),
            P(("row", "col"), None, None),
            P(("row", "col"), None),
            P(("row", "col")),
            P(("row", "col"), None),
        ),
        out_specs=P("row", None, "col"),
        check_vma=False,
    )
```

```python
import functools

import jax
import jax.numpy as jnp
from jax import lax
from jax.experimental import pallas as pl
from jax.experimental.pallas import tpu as pltpu
from jax.sharding import PartitionSpec as P

KC = 27
CR_SLAB = 16
MESH = pl.DeviceIdType.MESH
LANES = 128
GROUPS = 4
GROUP = 112
ROWS_STEP = 4
HALVES = ((0, 64), (64, 48))


def placement(rows, source, dest):
    row = lax.broadcasted_iota(jnp.int32, (rows, LANES), 0)
    lane = lax.broadcasted_iota(jnp.int32, (rows, LANES), 1)
    keep = (row - source == lane - dest) & (row >= source) & (row < source + 48)
    return jnp.where(keep, 1.0, 0.0).astype(jnp.bfloat16)


def move(value, matrix):
    return jnp.dot(value, matrix, preferred_element_type=jnp.float32).astype(jnp.bfloat16)


def gather_kernel(p_ref, out_ref, packed, send_sem, recv_sem):
    rows, width = p_ref.shape[0], p_ref.shape[1]
    half = rows // 2
    me = lax.axis_index("row")
    core, x = me % 2, me // 2
    other = x * 2 + 1 - core
    across = (1 - x) * 2 + core
    diagonal = (1 - x) * 2 + 1 - core

    barrier = pltpu.get_barrier_semaphore()
    for peer in (other, across):
        pl.semaphore_signal(barrier, inc=1, device_id={"row": peer}, device_id_type=MESH)

    low = p_ref[:half].reshape(half * width, width)
    high = p_ref[half:].reshape(half * width, width)
    first, second = placement(width, 0, 0), placement(width, 0, 48)
    both = jnp.dot(low, first, preferred_element_type=jnp.float32) + jnp.dot(
        high, second, preferred_element_type=jnp.float32
    )
    packed[0] = both.astype(jnp.bfloat16)
    pl.semaphore_wait(barrier, 2)

    def send(source, dest, peer):
        copy = pltpu.make_async_remote_copy(
            src_ref=packed.at[source],
            dst_ref=packed.at[dest],
            send_sem=send_sem.at[dest],
            recv_sem=recv_sem.at[dest],
            device_id={"row": peer},
            device_id_type=MESH,
        )
        copy.start()
        return copy

    def unpack(slot, owner):
        value = packed[slot]
        for side in range(2):
            for part in range(2):
                piece = move(value, placement(LANES, 48 * part, 64 * side))
                out_ref[side, pl.ds(owner * rows + half * part, half)] = piece.reshape(half, width, LANES)

    far = send(0, 2, across)
    near = send(0, 1, other)
    unpack(0, me)
    near.wait_recv()
    unpack(1, other)
    far.wait_recv()
    relay = send(2, 3, other)
    unpack(2, across)
    relay.wait_recv()
    unpack(3, diagonal)
    far.wait_send()
    near.wait_send()
    relay.wait_send()


def gather_rows(prolong, n_row):
    rows, width = prolong.shape[0], prolong.shape[1]
    return pl.pallas_call(
        gather_kernel,
        out_shape=jax.ShapeDtypeStruct((2, n_row * rows, width, LANES), jnp.bfloat16),
        in_specs=[pl.BlockSpec(memory_space=pltpu.VMEM)],
        out_specs=pl.BlockSpec(memory_space=pltpu.VMEM),
        scratch_shapes=[
            pltpu.VMEM((4, rows // 2 * width, LANES), jnp.bfloat16),
            pltpu.SemaphoreType.DMA((4,)),
            pltpu.SemaphoreType.DMA((4,)),
        ],
        compiler_params=pltpu.CompilerParams(
            collective_id=0, has_side_effects=True, vmem_limit_bytes=24 * 2**20
        ),
        name="gather_prolong",
    )(prolong)


def product_kernel(col_ref, slot_ref, agg_ref, tile_ref, own_ref, blk_ref, out_ref, acc):
    step = pl.program_id(0)
    width = own_ref.shape[1]
    neighbours = blk_ref.shape[1]

    @pl.when(step == 0)
    def _():
        @pl.loop(0, acc.shape[0] // 384)
        def _(at):
            acc[pl.ds(at * 384, 384), :] = jnp.zeros((384, LANES), jnp.float32)

    @pl.loop(0, ROWS_STEP)
    def _(r):
        i = step * ROWS_STEP + r
        turned = own_ref[i].astype(jnp.float32).T.astype(jnp.bfloat16)
        aggregate = agg_ref[i]
        blank = jnp.zeros((width, LANES), jnp.bfloat16)
        for first in range(0, neighbours, 4):
            group = range(first, min(first + 4, neighbours))
            left = jnp.concatenate([blk_ref[r, k] for k in group], axis=1)
            picked = [tile_ref[k % 4 % 2, col_ref[k, i]] for k in group]
            picked = [
                jnp.concatenate([p, blank] if at < 2 else [blank, p], axis=1) for at, p in enumerate(picked)
            ]
            product = jnp.dot(
                left, jnp.concatenate(picked, axis=0), preferred_element_type=jnp.float32
            ).astype(jnp.bfloat16)
            term = jnp.dot(turned, product, preferred_element_type=jnp.float32)
            for at, k in enumerate(group):
                value = term[:, at // 2 * LANES:(at // 2 + 1) * LANES]
                if at % 2:
                    value = pltpu.roll(value, 64, 1)
                base = pl.multiple_of((slot_ref[k, i] * CR_SLAB + aggregate) * width, width)
                acc[pl.ds(base, width), :] += value

    @pl.when(step == pl.num_programs(0) - 1)
    def _():
        lane = lax.broadcasted_iota(jnp.int32, (16, LANES), 1)

        @pl.loop(0, 8 * (GROUP // 16))
        def _(at):
            d, s = at // (GROUP // 16), at % (GROUP // 16)
            sums = [None] * 9
            for q in range(GROUPS):
                for r in range(6):
                    start = (GROUP * q + 16 * s) * width + 6 * d + r
                    offset = (q * 6 + r) * 48
                    j, shift = offset // LANES, offset % LANES
                    value = acc[pl.ds(start, 16, stride=width), :]
                    if shift:
                        value = pltpu.roll(value, shift, 1)
                    sums[j] = jnp.where(lane < shift, sums[j], value) if shift else value
                    if shift + 48 > LANES:
                        sums[j + 1] = value
            for j in range(9):
                out_ref[d, pl.ds(pl.multiple_of(16 * s, 16), 16), j * LANES:(j + 1) * LANES] = sums[j].astype(jnp.bfloat16)


def products(tile, prolong, blocks, columns, aggregate, slots):
    rows, neighbours, width = blocks.shape[0], blocks.shape[1], blocks.shape[2]
    smem = pl.BlockSpec(memory_space=pltpu.SMEM)
    vmem = pl.BlockSpec(memory_space=pltpu.VMEM)
    flops = rows * neighbours * width**3 * 4
    return pl.pallas_call(
        product_kernel,
        grid=(rows // ROWS_STEP,),
        out_shape=jax.ShapeDtypeStruct((8, GROUP, 9 * LANES), jnp.bfloat16),
        in_specs=[
            smem,
            smem,
            smem,
            vmem,
            vmem,
            pl.BlockSpec((ROWS_STEP, neighbours, width, width), lambda g: (g, 0, 0, 0)),
        ],
        out_specs=vmem,
        scratch_shapes=[pltpu.VMEM((GROUPS * GROUP * width, LANES), jnp.float32)],
        compiler_params=pltpu.CompilerParams(vmem_limit_bytes=40 * 2**20),
        cost_estimate=pl.CostEstimate(flops=flops, bytes_accessed=20 * 2**20, transcendentals=0),
        name="triple_products",
    )(columns.T, slots.T, aggregate, tile, prolong, blocks)


def scatter_kernel(x_ref, out_ref, ybuf, zsend, zbuf, own, ysend_sem, yrecv_sem, zsend_sem, zrecv_sem):
    me = lax.axis_index("col")
    y, z = me % 2, me // 2
    partner = z * 2 + 1 - y
    offsets = (2, 1, 3, 0)
    targets = [(z + offset) % 4 for offset in offsets]

    barrier = pltpu.get_barrier_semaphore()
    for peer in [partner] + [t * 2 + y for t in targets[:3]]:
        pl.semaphore_signal(barrier, inc=1, device_id={"col": peer}, device_id_type=MESH)
    pl.semaphore_wait(barrier, 4)

    ycopies, zcopies = {}, {}
    for s in range(4):
        for h, (begin, size) in enumerate(HALVES):
            copy = pltpu.make_async_remote_copy(
                src_ref=x_ref.at[targets[s] * 2 + 1 - y, pl.ds(begin, size)],
                dst_ref=ybuf.at[s, pl.ds(begin, size)],
                send_sem=ysend_sem.at[s, h],
                recv_sem=yrecv_sem.at[s, h],
                device_id={"col": partner},
                device_id_type=MESH,
            )
            copy.start()
            ycopies[s, h] = copy

    for s in range(4):
        for h, (begin, size) in enumerate(HALVES):
            ycopies[s, h].wait_recv()

            @pl.loop(begin // 16, (begin + size) // 16)
            def _(at):
                rows = pl.ds(pl.multiple_of(at * 16, 16), 16)
                total = x_ref[targets[s] * 2 + y, rows, :].astype(jnp.float32) + ybuf[s, rows, :].astype(jnp.float32)
                if s < 3:
                    zsend[s, rows, :] = total.astype(jnp.bfloat16)
                else:
                    own[rows, :] = total

            if s < 3:
                copy = pltpu.make_async_remote_copy(
                    src_ref=zsend.at[s, pl.ds(begin, size)],
                    dst_ref=zbuf.at[s, pl.ds(begin, size)],
                    send_sem=zsend_sem.at[s, h],
                    recv_sem=zrecv_sem.at[s, h],
                    device_id={"col": targets[s] * 2 + y},
                    device_id_type=MESH,
                )
                copy.start()
                zcopies[s, h] = copy

    for copy in zcopies.values():
        copy.wait_recv()

    lane = lax.broadcasted_iota(jnp.int32, (16, LANES), 1)

    def unpack(at, groups):
        rows = pl.ds(pl.multiple_of(at * 16, 16), 16)
        total = own[rows, :]
        for s in range(3):
            total = total + zbuf[s, rows, :].astype(jnp.float32)
        for q in range(groups):
            j, shift = 288 * q // LANES, 288 * q % LANES
            turned = [total[:, (j + m) * LANES:(j + m + 1) * LANES] for m in range(3)]
            if shift:
                turned = [pltpu.roll(piece, LANES - shift, 1) for piece in turned]
            target = pl.ds(pl.multiple_of(GROUP * q + at * 16, 16), 16)
            for m in range(2):
                piece = turned[m]
                if shift:
                    piece = jnp.where(lane < LANES - shift, piece, turned[m + 1])
                out_ref[target, m * LANES:(m + 1) * LANES] = piece
            out_ref[target, 256:288] = turned[2][:, :32]

    @pl.loop(0, 6)
    def _(at):
        unpack(at, 4)

    unpack(6, 3)

    for copy in list(ycopies.values()) + list(zcopies.values()):
        copy.wait_send()


def scatter_cols(packed):
    half = len(HALVES)
    return pl.pallas_call(
        scatter_kernel,
        out_shape=jax.ShapeDtypeStruct((KC * CR_SLAB, 288), jnp.float32),
        in_specs=[pl.BlockSpec(memory_space=pltpu.VMEM)],
        out_specs=pl.BlockSpec(memory_space=pltpu.VMEM),
        scratch_shapes=[
            pltpu.VMEM((4, GROUP, 9 * LANES), jnp.bfloat16),
            pltpu.VMEM((3, GROUP, 9 * LANES), jnp.bfloat16),
            pltpu.VMEM((3, GROUP, 9 * LANES), jnp.bfloat16),
            pltpu.VMEM((GROUP, 9 * LANES), jnp.float32),
            pltpu.SemaphoreType.DMA((4, half)),
            pltpu.SemaphoreType.DMA((4, half)),
            pltpu.SemaphoreType.DMA((3, half)),
            pltpu.SemaphoreType.DMA((3, half)),
        ],
        compiler_params=pltpu.CompilerParams(
            collective_id=1, has_side_effects=True, vmem_limit_bytes=24 * 2**20
        ),
        name="scatter_cols",
    )(packed)


def shards(n_row, blocks, prolong, columns, aggregate, slots):
    tile = gather_rows(prolong, n_row)
    packed = products(tile, prolong, blocks, columns, aggregate, slots)
    result = scatter_cols(packed)
    return result.reshape(KC, CR_SLAB, 288).transpose(1, 0, 2)


def shards_any(blocks, prolong, columns, aggregate, slots):
    width = blocks.shape[2]
    tile = lax.all_gather(prolong, "row", axis=0, tiled=True)
    picked = jnp.take(tile, columns, axis=0)
    product = jnp.einsum(
        "rkab,rkbc->rkac", blocks, picked, preferred_element_type=jnp.float32
    ).astype(jnp.bfloat16)
    term = jnp.einsum("rba,rkbc->rkac", prolong, product, preferred_element_type=jnp.float32)
    target = (aggregate[:, None] * KC + slots).reshape(-1)
    partial_value = jax.ops.segment_sum(
        term.reshape(-1, width * width), target, num_segments=CR_SLAB * KC
    )
    partial_value = partial_value.reshape(CR_SLAB, KC, width * width)
    summed = lax.psum(partial_value, "col")
    share = width * width // lax.axis_size("col")
    return lax.dynamic_slice_in_dim(summed, lax.axis_index("col") * share, share, 2)


def solution(mesh):
    n_row, n_col = mesh.shape["row"], mesh.shape["col"]
    body = functools.partial(shards, n_row) if (n_row, n_col) == (4, 8) else shards_any
    return jax.shard_map(
        body,
        mesh=mesh,
        in_specs=(
            P(("row", "col"), None, None, None),
            P(("row", "col"), None, None),
            P(("row", "col"), None),
            P(("row", "col")),
            P(("row", "col"), None),
        ),
        out_specs=P("row", None, "col"),
        check_vma=False,
    )
```

```python
import functools

import jax
import jax.numpy as jnp
from jax import lax
from jax.experimental import pallas as pl
from jax.experimental.pallas import tpu as pltpu
from jax.sharding import PartitionSpec as P

KC = 27
CR_SLAB = 16
MESH = pl.DeviceIdType.MESH
LANES = 128
GROUPS = 4
GROUP = 112
ROWS_STEP = 4
PARTS = 3
HALVES = ((0, 64), (64, 48))


def placement(rows, source, dest):
    row = lax.broadcasted_iota(jnp.int32, (rows, LANES), 0)
    lane = lax.broadcasted_iota(jnp.int32, (rows, LANES), 1)
    keep = (row - source == lane - dest) & (row >= source) & (row < source + 48)
    return jnp.where(keep, 1.0, 0.0).astype(jnp.bfloat16)


def move(value, matrix):
    return jnp.dot(value, matrix, preferred_element_type=jnp.float32).astype(jnp.bfloat16)


def gather_kernel(p_ref, out_ref, packed, send_sem, recv_sem):
    rows, width = p_ref.shape[0], p_ref.shape[1]
    half = rows // 2
    me = lax.axis_index("row")
    core, x = me % 2, me // 2
    other = x * 2 + 1 - core
    across = (1 - x) * 2 + core
    diagonal = (1 - x) * 2 + 1 - core

    barrier = pltpu.get_barrier_semaphore()
    for peer in (other, across):
        pl.semaphore_signal(barrier, inc=1, device_id={"row": peer}, device_id_type=MESH)

    low = p_ref[:half].reshape(half * width, width)
    high = p_ref[half:].reshape(half * width, width)
    first, second = placement(width, 0, 0), placement(width, 0, 48)
    both = jnp.dot(low, first, preferred_element_type=jnp.float32) + jnp.dot(
        high, second, preferred_element_type=jnp.float32
    )
    packed[0] = both.astype(jnp.bfloat16)
    pl.semaphore_wait(barrier, 2)

    def send(source, dest, peer):
        copy = pltpu.make_async_remote_copy(
            src_ref=packed.at[source],
            dst_ref=packed.at[dest],
            send_sem=send_sem.at[dest],
            recv_sem=recv_sem.at[dest],
            device_id={"row": peer},
            device_id_type=MESH,
        )
        copy.start()
        return copy

    def unpack(slot, owner):
        value = packed[slot]
        out_ref[pl.ds(owner * rows, half)] = move(value, placement(LANES, 0, 0)).reshape(half, width, LANES)
        out_ref[pl.ds(owner * rows + half, half)] = move(value, placement(LANES, 48, 0)).reshape(half, width, LANES)

    far = send(0, 2, across)
    near = send(0, 1, other)
    unpack(0, me)
    near.wait_recv()
    unpack(1, other)
    far.wait_recv()
    relay = send(2, 3, other)
    unpack(2, across)
    relay.wait_recv()
    unpack(3, diagonal)
    far.wait_send()
    near.wait_send()
    relay.wait_send()


def gather_rows(prolong, n_row):
    rows, width = prolong.shape[0], prolong.shape[1]
    return pl.pallas_call(
        gather_kernel,
        out_shape=jax.ShapeDtypeStruct((n_row * rows, width, LANES), jnp.bfloat16),
        in_specs=[pl.BlockSpec(memory_space=pltpu.VMEM)],
        out_specs=pl.BlockSpec(memory_space=pltpu.VMEM),
        scratch_shapes=[
            pltpu.VMEM((4, rows // 2 * width, LANES), jnp.bfloat16),
            pltpu.SemaphoreType.DMA((4,)),
            pltpu.SemaphoreType.DMA((4,)),
        ],
        compiler_params=pltpu.CompilerParams(
            collective_id=0, has_side_effects=True, vmem_limit_bytes=24 * 2**20
        ),
        name="gather_prolong",
    )(prolong)


def product_kernel(col_ref, slot_ref, agg_ref, tile_ref, own_ref, blk_ref, out_ref, acc):
    step = pl.program_id(0)
    width = own_ref.shape[1]
    neighbours = blk_ref.shape[1]

    @pl.when(step == 0)
    def _():
        @pl.loop(0, acc.shape[0] // 384)
        def _(at):
            acc[pl.ds(at * 384, 384), :] = jnp.zeros((384, LANES), jnp.float32)

    def one_row(r):
        i = step * ROWS_STEP + r
        turned = own_ref[i]
        aggregate = agg_ref[i]
        for first in range(0, neighbours, 2):
            group = range(first, min(first + 2, neighbours))
            product = [
                jnp.dot(
                    blk_ref[r, k], tile_ref[col_ref[k, i]], preferred_element_type=jnp.float32
                ).astype(jnp.bfloat16)
                for k in group
            ]
            term = jnp.dot(turned, jnp.concatenate(product, axis=1), preferred_element_type=jnp.float32)
            for at, k in enumerate(group):
                base = pl.multiple_of((slot_ref[k, i] * CR_SLAB + aggregate) * width, width)
                acc[pl.ds(base, width), :] += term[:, at * LANES:(at + 1) * LANES]

    @pl.loop(0, ROWS_STEP // 2)
    def _(at):
        one_row(at * 2)
        one_row(at * 2 + 1)

    @pl.when(step == pl.num_programs(0) - 1)
    def _():
        lane = lax.broadcasted_iota(jnp.int32, (16, LANES), 1)

        @pl.loop(0, 8 * (GROUP // 16))
        def _(at):
            d, s = at // (GROUP // 16), at % (GROUP // 16)
            sums = [None] * 9
            for q in range(GROUPS):
                for r in range(6):
                    start = (GROUP * q + 16 * s) * width + 6 * d + r
                    offset = (q * 6 + r) * 48
                    j, shift = offset // LANES, offset % LANES
                    value = acc[pl.ds(start, 16, stride=width), :]
                    if shift:
                        value = pltpu.roll(value, shift, 1)
                    over = shift + 48 - LANES
                    if over > 0:
                        spill = jnp.where(lane < over, value, 0.0)
                        value = jnp.where(lane < over, 0.0, value)
                        sums[j + 1] = spill
                    sums[j] = value if sums[j] is None else sums[j] + value
            for j in range(9):
                out_ref[d, pl.ds(pl.multiple_of(16 * s, 16), 16), j * LANES:(j + 1) * LANES] = sums[j].astype(jnp.bfloat16)


def products(tile, turned, blocks, columns, aggregate, slots):
    rows, neighbours, width = blocks.shape[0], blocks.shape[1], blocks.shape[2]
    smem = pl.BlockSpec(memory_space=pltpu.SMEM)
    vmem = pl.BlockSpec(memory_space=pltpu.VMEM)
    flops = rows * neighbours * width**3 * 4
    return pl.pallas_call(
        product_kernel,
        grid=(rows // ROWS_STEP,),
        out_shape=jax.ShapeDtypeStruct((8, GROUP, 9 * LANES), jnp.bfloat16),
        in_specs=[
            smem,
            smem,
            smem,
            vmem,
            vmem,
            pl.BlockSpec((ROWS_STEP, neighbours, width, width), lambda g: (g, 0, 0, 0)),
        ],
        out_specs=vmem,
        scratch_shapes=[pltpu.VMEM((GROUPS * GROUP * width, LANES), jnp.float32)],
        compiler_params=pltpu.CompilerParams(vmem_limit_bytes=40 * 2**20),
        cost_estimate=pl.CostEstimate(flops=flops, bytes_accessed=20 * 2**20, transcendentals=0),
        name="triple_products",
    )(columns.T, slots.T, aggregate, tile, turned, blocks)


def scatter_kernel(x_ref, out_ref, ybuf, zsend, zbuf, own, ysend_sem, yrecv_sem, zsend_sem, zrecv_sem):
    me = lax.axis_index("col")
    y, z = me % 2, me // 2
    partner = z * 2 + 1 - y
    offsets = (2, 1, 3, 0)
    targets = [(z + offset) % 4 for offset in offsets]

    barrier = pltpu.get_barrier_semaphore()
    for peer in [partner] + [t * 2 + y for t in targets[:3]]:
        pl.semaphore_signal(barrier, inc=1, device_id={"col": peer}, device_id_type=MESH)
    pl.semaphore_wait(barrier, 4)

    ycopies, zcopies = {}, {}
    for s in range(4):
        for h, (begin, size) in enumerate(HALVES):
            copy = pltpu.make_async_remote_copy(
                src_ref=x_ref.at[targets[s] * 2 + 1 - y, pl.ds(begin, size)],
                dst_ref=ybuf.at[s, pl.ds(begin, size)],
                send_sem=ysend_sem.at[s, h],
                recv_sem=yrecv_sem.at[s, h],
                device_id={"col": partner},
                device_id_type=MESH,
            )
            copy.start()
            ycopies[s, h] = copy

    for s in range(4):
        for h, (begin, size) in enumerate(HALVES):
            ycopies[s, h].wait_recv()

            @pl.loop(begin // 16, (begin + size) // 16)
            def _(at):
                rows = pl.ds(pl.multiple_of(at * 16, 16), 16)
                total = x_ref[targets[s] * 2 + y, rows, :].astype(jnp.float32) + ybuf[s, rows, :].astype(jnp.float32)
                if s < 3:
                    zsend[s, rows, :] = total.astype(jnp.bfloat16)
                else:
                    own[rows, :] = total

            if s < 3:
                copy = pltpu.make_async_remote_copy(
                    src_ref=zsend.at[s, pl.ds(begin, size)],
                    dst_ref=zbuf.at[s, pl.ds(begin, size)],
                    send_sem=zsend_sem.at[s, h],
                    recv_sem=zrecv_sem.at[s, h],
                    device_id={"col": targets[s] * 2 + y},
                    device_id_type=MESH,
                )
                copy.start()
                zcopies[s, h] = copy

    for copy in zcopies.values():
        copy.wait_recv()

    lane = lax.broadcasted_iota(jnp.int32, (16, LANES), 1)

    def unpack(at, groups):
        rows = pl.ds(pl.multiple_of(at * 16, 16), 16)
        total = own[rows, :]
        for s in range(3):
            total = total + zbuf[s, rows, :].astype(jnp.float32)
        for q in range(groups):
            j, shift = 288 * q // LANES, 288 * q % LANES
            turned = [total[:, (j + m) * LANES:(j + m + 1) * LANES] for m in range(3)]
            if shift:
                turned = [pltpu.roll(piece, LANES - shift, 1) for piece in turned]
            target = pl.ds(pl.multiple_of(GROUP * q + at * 16, 16), 16)
            for m in range(2):
                piece = turned[m]
                if shift:
                    piece = jnp.where(lane < LANES - shift, piece, turned[m + 1])
                out_ref[target, m * LANES:(m + 1) * LANES] = piece
            out_ref[target, 256:288] = turned[2][:, :32]

    @pl.loop(0, 6)
    def _(at):
        unpack(at, 4)

    unpack(6, 3)

    for copy in list(ycopies.values()) + list(zcopies.values()):
        copy.wait_send()


def scatter_cols(packed):
    half = len(HALVES)
    return pl.pallas_call(
        scatter_kernel,
        out_shape=jax.ShapeDtypeStruct((KC * CR_SLAB, 288), jnp.float32),
        in_specs=[pl.BlockSpec(memory_space=pltpu.VMEM)],
        out_specs=pl.BlockSpec(memory_space=pltpu.VMEM),
        scratch_shapes=[
            pltpu.VMEM((4, GROUP, 9 * LANES), jnp.bfloat16),
            pltpu.VMEM((3, GROUP, 9 * LANES), jnp.bfloat16),
            pltpu.VMEM((3, GROUP, 9 * LANES), jnp.bfloat16),
            pltpu.VMEM((GROUP, 9 * LANES), jnp.float32),
            pltpu.SemaphoreType.DMA((4, half)),
            pltpu.SemaphoreType.DMA((4, half)),
            pltpu.SemaphoreType.DMA((3, half)),
            pltpu.SemaphoreType.DMA((3, half)),
        ],
        compiler_params=pltpu.CompilerParams(
            collective_id=1, has_side_effects=True, vmem_limit_bytes=24 * 2**20
        ),
        name="scatter_cols",
    )(packed)


def shards(n_row, blocks, prolong, columns, aggregate, slots):
    tile = gather_rows(prolong, n_row)
    turned = jnp.swapaxes(prolong, 1, 2)
    packed = products(tile, turned, blocks, columns, aggregate, slots)
    result = scatter_cols(packed)
    return result.reshape(KC, CR_SLAB, 288).transpose(1, 0, 2)


def shards_any(blocks, prolong, columns, aggregate, slots):
    width = blocks.shape[2]
    tile = lax.all_gather(prolong, "row", axis=0, tiled=True)
    picked = jnp.take(tile, columns, axis=0)
    product = jnp.einsum(
        "rkab,rkbc->rkac", blocks, picked, preferred_element_type=jnp.float32
    ).astype(jnp.bfloat16)
    term = jnp.einsum("rba,rkbc->rkac", prolong, product, preferred_element_type=jnp.float32)
    target = (aggregate[:, None] * KC + slots).reshape(-1)
    partial_value = jax.ops.segment_sum(
        term.reshape(-1, width * width), target, num_segments=CR_SLAB * KC
    )
    partial_value = partial_value.reshape(CR_SLAB, KC, width * width)
    summed = lax.psum(partial_value, "col")
    share = width * width // lax.axis_size("col")
    return lax.dynamic_slice_in_dim(summed, lax.axis_index("col") * share, share, 2)


def solution(mesh):
    n_row, n_col = mesh.shape["row"], mesh.shape["col"]
    body = functools.partial(shards, n_row) if (n_row, n_col) == (4, 8) else shards_any
    return jax.shard_map(
        body,
        mesh=mesh,
        in_specs=(
            P(("row", "col"), None, None, None),
            P(("row", "col"), None, None),
            P(("row", "col"), None),
            P(("row", "col")),
            P(("row", "col"), None),
        ),
        out_specs=P("row", None, "col"),
        check_vma=False,
    )
```

```python
import functools

import jax
import jax.numpy as jnp
from jax import lax
from jax.experimental import pallas as pl
from jax.experimental.pallas import tpu as pltpu
from jax.sharding import PartitionSpec as P

KC = 27
CR_SLAB = 16
MESH = pl.DeviceIdType.MESH
LANES = 128
GROUPS = 4
GROUP = 112
ROWS_STEP = 4
PARTS = 3
HALVES = ((0, 64), (64, 48))


def placement(rows, source, dest):
    row = lax.broadcasted_iota(jnp.int32, (rows, LANES), 0)
    lane = lax.broadcasted_iota(jnp.int32, (rows, LANES), 1)
    keep = (row - source == lane - dest) & (row >= source) & (row < source + 48)
    return jnp.where(keep, 1.0, 0.0).astype(jnp.bfloat16)


def move(value, matrix):
    return jnp.dot(value, matrix, preferred_element_type=jnp.float32).astype(jnp.bfloat16)


def gather_kernel(p_ref, out_ref, packed, send_sem, recv_sem):
    rows, width = p_ref.shape[0], p_ref.shape[1]
    half = rows // 2
    me = lax.axis_index("row")
    core, x = me % 2, me // 2
    other = x * 2 + 1 - core
    across = (1 - x) * 2 + core
    diagonal = (1 - x) * 2 + 1 - core

    barrier = pltpu.get_barrier_semaphore()
    for peer in (other, across):
        pl.semaphore_signal(barrier, inc=1, device_id={"row": peer}, device_id_type=MESH)

    low = p_ref[:half].reshape(half * width, width)
    high = p_ref[half:].reshape(half * width, width)
    first, second = placement(width, 0, 0), placement(width, 0, 48)
    both = jnp.dot(low, first, preferred_element_type=jnp.float32) + jnp.dot(
        high, second, preferred_element_type=jnp.float32
    )
    packed[0] = both.astype(jnp.bfloat16)
    pl.semaphore_wait(barrier, 2)

    step = half * width // PARTS
    blocks = half // PARTS

    def send(source, dest, part, peer):
        copy = pltpu.make_async_remote_copy(
            src_ref=packed.at[source, pl.ds(part * step, step)],
            dst_ref=packed.at[dest, pl.ds(part * step, step)],
            send_sem=send_sem.at[dest, part],
            recv_sem=recv_sem.at[dest, part],
            device_id={"row": peer},
            device_id_type=MESH,
        )
        copy.start()
        return copy

    def unpack(slot, part, owner):
        value = packed[slot, pl.ds(part * step, step), :]
        for side in range(2):
            at = owner * rows + half * side + part * blocks
            piece = move(value, placement(LANES, 48 * side, 0))
            out_ref[pl.ds(at, blocks)] = piece.reshape(blocks, width, LANES)

    far = [send(0, 2, part, across) for part in range(PARTS)]
    near = [send(0, 1, part, other) for part in range(PARTS)]
    for part in range(PARTS):
        unpack(0, part, me)
    for part in range(PARTS):
        near[part].wait_recv()
        unpack(1, part, other)
    relay = []
    for part in range(PARTS):
        far[part].wait_recv()
        relay.append(send(2, 3, part, other))
        unpack(2, part, across)
    for part in range(PARTS):
        relay[part].wait_recv()
        unpack(3, part, diagonal)
    for copy in far + near + relay:
        copy.wait_send()


def gather_rows(prolong, n_row):
    rows, width = prolong.shape[0], prolong.shape[1]
    return pl.pallas_call(
        gather_kernel,
        out_shape=jax.ShapeDtypeStruct((n_row * rows, width, LANES), jnp.bfloat16),
        in_specs=[pl.BlockSpec(memory_space=pltpu.VMEM)],
        out_specs=pl.BlockSpec(memory_space=pltpu.VMEM),
        scratch_shapes=[
            pltpu.VMEM((4, rows // 2 * width, LANES), jnp.bfloat16),
            pltpu.SemaphoreType.DMA((4, PARTS)),
            pltpu.SemaphoreType.DMA((4, PARTS)),
        ],
        compiler_params=pltpu.CompilerParams(
            collective_id=0, has_side_effects=True, vmem_limit_bytes=24 * 2**20
        ),
        name="gather_prolong",
    )(prolong)


def product_kernel(col_ref, slot_ref, agg_ref, tile_ref, own_ref, blk_ref, out_ref, acc, product, term, turned):
    step = pl.program_id(0)
    width = own_ref.shape[1]
    neighbours = blk_ref.shape[1]

    @pl.when(step == 0)
    def _():
        @pl.loop(0, acc.shape[0] // 384)
        def _(at):
            acc[pl.ds(at * 384, 384), :] = jnp.zeros((384, LANES), jnp.float32)

        product[...] = jnp.zeros_like(product)
        term[...] = jnp.zeros_like(term)
        turned[...] = jnp.zeros_like(turned)

    last = own_ref.shape[0] - 1

    def add_term(i, k):
        base = pl.multiple_of((slot_ref[i, k] * CR_SLAB + agg_ref[i]) * width, width)
        acc[pl.ds(base, width), :] += term[k]

    def second(k):
        term[k] = jnp.dot(turned[...], product[k], preferred_element_type=jnp.float32)

    @pl.loop(0, ROWS_STEP)
    def _(r):
        i = step * ROWS_STEP + r
        before = jnp.maximum(i - 2, 0)
        for k in range(neighbours):
            add_term(before, k)
            second(k)
            product[k] = jnp.dot(
                blk_ref[r, k], tile_ref[col_ref[i, k]], preferred_element_type=jnp.float32
            ).astype(jnp.bfloat16)
        turned[...] = own_ref[i].astype(jnp.float32).T.astype(jnp.bfloat16)

    @pl.when(step == pl.num_programs(0) - 1)
    def _():
        for k in range(neighbours):
            add_term(last - 1, k)
            second(k)
        for k in range(neighbours):
            add_term(last, k)

    @pl.when(step == pl.num_programs(0) - 1)
    def _():
        lane = lax.broadcasted_iota(jnp.int32, (16, LANES), 1)

        @pl.loop(0, 8 * (GROUP // 16))
        def _(at):
            d, s = at // (GROUP // 16), at % (GROUP // 16)
            sums = [None] * 9
            for q in range(GROUPS):
                for r in range(6):
                    start = (GROUP * q + 16 * s) * width + 6 * d + r
                    offset = (q * 6 + r) * 48
                    j, shift = offset // LANES, offset % LANES
                    value = acc[pl.ds(start, 16, stride=width), :]
                    if shift:
                        value = pltpu.roll(value, shift, 1)
                    over = shift + 48 - LANES
                    if over > 0:
                        spill = jnp.where(lane < over, value, 0.0)
                        value = jnp.where(lane < over, 0.0, value)
                        sums[j + 1] = spill
                    sums[j] = value if sums[j] is None else sums[j] + value
            for j in range(9):
                out_ref[d, pl.ds(pl.multiple_of(16 * s, 16), 16), j * LANES:(j + 1) * LANES] = sums[j].astype(jnp.bfloat16)


def products(tile, prolong, blocks, columns, aggregate, slots):
    rows, neighbours, width = blocks.shape[0], blocks.shape[1], blocks.shape[2]
    smem = pl.BlockSpec(memory_space=pltpu.SMEM)
    vmem = pl.BlockSpec(memory_space=pltpu.VMEM)
    flops = rows * neighbours * width**3 * 4
    return pl.pallas_call(
        product_kernel,
        grid=(rows // ROWS_STEP,),
        out_shape=jax.ShapeDtypeStruct((8, GROUP, 9 * LANES), jnp.bfloat16),
        in_specs=[
            smem,
            smem,
            smem,
            vmem,
            vmem,
            pl.BlockSpec((ROWS_STEP, neighbours, width, width), lambda g: (g, 0, 0, 0)),
        ],
        out_specs=vmem,
        scratch_shapes=[
            pltpu.VMEM((GROUPS * GROUP * width, LANES), jnp.float32),
            pltpu.VMEM((neighbours, width, LANES), jnp.bfloat16),
            pltpu.VMEM((neighbours, width, LANES), jnp.float32),
            pltpu.VMEM((width, width), jnp.bfloat16),
        ],
        compiler_params=pltpu.CompilerParams(vmem_limit_bytes=40 * 2**20),
        cost_estimate=pl.CostEstimate(flops=flops, bytes_accessed=20 * 2**20, transcendentals=0),
        name="triple_products",
    )(columns, slots, aggregate, tile, prolong, blocks)


def scatter_kernel(x_ref, out_ref, ybuf, zsend, zbuf, own, ysend_sem, yrecv_sem, zsend_sem, zrecv_sem):
    me = lax.axis_index("col")
    y, z = me % 2, me // 2
    partner = z * 2 + 1 - y
    offsets = (2, 1, 3, 0)
    targets = [(z + offset) % 4 for offset in offsets]

    barrier = pltpu.get_barrier_semaphore()
    for peer in [partner] + [t * 2 + y for t in targets[:3]]:
        pl.semaphore_signal(barrier, inc=1, device_id={"col": peer}, device_id_type=MESH)
    pl.semaphore_wait(barrier, 4)

    ycopies, zcopies = {}, {}
    for s in range(4):
        for h, (begin, size) in enumerate(HALVES):
            copy = pltpu.make_async_remote_copy(
                src_ref=x_ref.at[targets[s] * 2 + 1 - y, pl.ds(begin, size)],
                dst_ref=ybuf.at[s, pl.ds(begin, size)],
                send_sem=ysend_sem.at[s, h],
                recv_sem=yrecv_sem.at[s, h],
                device_id={"col": partner},
                device_id_type=MESH,
            )
            copy.start()
            ycopies[s, h] = copy

    for s in range(4):
        for h, (begin, size) in enumerate(HALVES):
            ycopies[s, h].wait_recv()

            @pl.loop(begin // 16, (begin + size) // 16)
            def _(at):
                rows = pl.ds(pl.multiple_of(at * 16, 16), 16)
                total = x_ref[targets[s] * 2 + y, rows, :].astype(jnp.float32) + ybuf[s, rows, :].astype(jnp.float32)
                if s < 3:
                    zsend[s, rows, :] = total.astype(jnp.bfloat16)
                else:
                    own[rows, :] = total

            if s < 3:
                copy = pltpu.make_async_remote_copy(
                    src_ref=zsend.at[s, pl.ds(begin, size)],
                    dst_ref=zbuf.at[s, pl.ds(begin, size)],
                    send_sem=zsend_sem.at[s, h],
                    recv_sem=zrecv_sem.at[s, h],
                    device_id={"col": targets[s] * 2 + y},
                    device_id_type=MESH,
                )
                copy.start()
                zcopies[s, h] = copy

    for copy in zcopies.values():
        copy.wait_recv()

    lane = lax.broadcasted_iota(jnp.int32, (16, LANES), 1)

    def unpack(at, groups):
        rows = pl.ds(pl.multiple_of(at * 16, 16), 16)
        total = own[rows, :]
        for s in range(3):
            total = total + zbuf[s, rows, :].astype(jnp.float32)
        for q in range(groups):
            j, shift = 288 * q // LANES, 288 * q % LANES
            turned = [total[:, (j + m) * LANES:(j + m + 1) * LANES] for m in range(3)]
            if shift:
                turned = [pltpu.roll(piece, LANES - shift, 1) for piece in turned]
            target = pl.ds(pl.multiple_of(GROUP * q + at * 16, 16), 16)
            for m in range(2):
                piece = turned[m]
                if shift:
                    piece = jnp.where(lane < LANES - shift, piece, turned[m + 1])
                out_ref[target, m * LANES:(m + 1) * LANES] = piece
            out_ref[target, 256:288] = turned[2][:, :32]

    @pl.loop(0, 6)
    def _(at):
        unpack(at, 4)

    unpack(6, 3)

    for copy in list(ycopies.values()) + list(zcopies.values()):
        copy.wait_send()


def scatter_cols(packed):
    half = len(HALVES)
    return pl.pallas_call(
        scatter_kernel,
        out_shape=jax.ShapeDtypeStruct((KC * CR_SLAB, 288), jnp.float32),
        in_specs=[pl.BlockSpec(memory_space=pltpu.VMEM)],
        out_specs=pl.BlockSpec(memory_space=pltpu.VMEM),
        scratch_shapes=[
            pltpu.VMEM((4, GROUP, 9 * LANES), jnp.bfloat16),
            pltpu.VMEM((3, GROUP, 9 * LANES), jnp.bfloat16),
            pltpu.VMEM((3, GROUP, 9 * LANES), jnp.bfloat16),
            pltpu.VMEM((GROUP, 9 * LANES), jnp.float32),
            pltpu.SemaphoreType.DMA((4, half)),
            pltpu.SemaphoreType.DMA((4, half)),
            pltpu.SemaphoreType.DMA((3, half)),
            pltpu.SemaphoreType.DMA((3, half)),
        ],
        compiler_params=pltpu.CompilerParams(
            collective_id=1, has_side_effects=True, vmem_limit_bytes=24 * 2**20
        ),
        name="scatter_cols",
    )(packed)


def shards(n_row, blocks, prolong, columns, aggregate, slots):
    tile = gather_rows(prolong, n_row)
    packed = products(tile, prolong, blocks, columns, aggregate, slots)
    result = scatter_cols(packed)
    return result.reshape(KC, CR_SLAB, 288).transpose(1, 0, 2)


def shards_any(blocks, prolong, columns, aggregate, slots):
    width = blocks.shape[2]
    tile = lax.all_gather(prolong, "row", axis=0, tiled=True)
    picked = jnp.take(tile, columns, axis=0)
    product = jnp.einsum(
        "rkab,rkbc->rkac", blocks, picked, preferred_element_type=jnp.float32
    ).astype(jnp.bfloat16)
    term = jnp.einsum("rba,rkbc->rkac", prolong, product, preferred_element_type=jnp.float32)
    target = (aggregate[:, None] * KC + slots).reshape(-1)
    partial_value = jax.ops.segment_sum(
        term.reshape(-1, width * width), target, num_segments=CR_SLAB * KC
    )
    partial_value = partial_value.reshape(CR_SLAB, KC, width * width)
    summed = lax.psum(partial_value, "col")
    share = width * width // lax.axis_size("col")
    return lax.dynamic_slice_in_dim(summed, lax.axis_index("col") * share, share, 2)


def solution(mesh):
    n_row, n_col = mesh.shape["row"], mesh.shape["col"]
    body = functools.partial(shards, n_row) if (n_row, n_col) == (4, 8) else shards_any
    return jax.shard_map(
        body,
        mesh=mesh,
        in_specs=(
            P(("row", "col"), None, None, None),
            P(("row", "col"), None, None),
            P(("row", "col"), None),
            P(("row", "col")),
            P(("row", "col"), None),
        ),
        out_specs=P("row", None, "col"),
        check_vma=False,
    )
```

```python
import functools

import jax
import jax.numpy as jnp
from jax import lax
from jax.experimental import pallas as pl
from jax.experimental.pallas import tpu as pltpu
from jax.sharding import PartitionSpec as P

KC = 27
CR_SLAB = 16
MESH = pl.DeviceIdType.MESH
LANES = 128
GROUPS = 4
GROUP = 112
ROWS_STEP = 4
PARTS = 3
CHUNK = 9
HALVES = ((0, 64), (64, 48))


def placement(rows, source, dest):
    row = lax.broadcasted_iota(jnp.int32, (rows, LANES), 0)
    lane = lax.broadcasted_iota(jnp.int32, (rows, LANES), 1)
    keep = (row - source == lane - dest) & (row >= source) & (row < source + 48)
    return jnp.where(keep, 1.0, 0.0).astype(jnp.bfloat16)


def move(value, matrix):
    return jnp.dot(value, matrix, preferred_element_type=jnp.float32).astype(jnp.bfloat16)


def gather_kernel(p_ref, out_ref, turned, packed, send_sem, recv_sem):
    rows, width = p_ref.shape[0], p_ref.shape[1]
    half = rows // 2
    me = lax.axis_index("row")
    core, x = me % 2, me // 2
    other = x * 2 + 1 - core
    across = (1 - x) * 2 + core
    diagonal = (1 - x) * 2 + 1 - core

    barrier = pltpu.get_barrier_semaphore()
    for peer in (other, across):
        pl.semaphore_signal(barrier, inc=1, device_id={"row": peer}, device_id_type=MESH)

    @pl.loop(0, rows // 8)
    def _(at):
        for n in range(8):
            turned[at * 8 + n] = p_ref[at * 8 + n].astype(jnp.float32).T.astype(jnp.bfloat16)

    low = turned[:half].reshape(half * width, width)
    high = turned[half:].reshape(half * width, width)
    first, second = placement(width, 0, 0), placement(width, 0, 48)
    both = jnp.dot(low, first, preferred_element_type=jnp.float32) + jnp.dot(
        high, second, preferred_element_type=jnp.float32
    )
    packed[0] = both.astype(jnp.bfloat16)
    pl.semaphore_wait(barrier, 2)

    step = half * width // PARTS
    blocks = half // PARTS

    def send(source, dest, part, peer):
        copy = pltpu.make_async_remote_copy(
            src_ref=packed.at[source, pl.ds(part * step, step)],
            dst_ref=packed.at[dest, pl.ds(part * step, step)],
            send_sem=send_sem.at[dest, part],
            recv_sem=recv_sem.at[dest, part],
            device_id={"row": peer},
            device_id_type=MESH,
        )
        copy.start()
        return copy

    def unpack(slot, part, owner):
        value = packed[slot, pl.ds(part * step, step), :]
        for side in range(2):
            at = owner * rows + half * side + part * blocks
            piece = move(value, placement(LANES, 48 * side, 0))
            out_ref[pl.ds(at, blocks)] = piece.reshape(blocks, width, LANES)

    far = [send(0, 2, part, across) for part in range(PARTS)]
    near = [send(0, 1, part, other) for part in range(PARTS)]
    for part in range(PARTS):
        unpack(0, part, me)
    for part in range(PARTS):
        near[part].wait_recv()
        unpack(1, part, other)
    relay = []
    for part in range(PARTS):
        far[part].wait_recv()
        relay.append(send(2, 3, part, other))
        unpack(2, part, across)
    for part in range(PARTS):
        relay[part].wait_recv()
        unpack(3, part, diagonal)
    for copy in far + near + relay:
        copy.wait_send()


def gather_rows(prolong, n_row):
    rows, width = prolong.shape[0], prolong.shape[1]
    return pl.pallas_call(
        gather_kernel,
        out_shape=jax.ShapeDtypeStruct((n_row * rows, width, LANES), jnp.bfloat16),
        in_specs=[pl.BlockSpec(memory_space=pltpu.VMEM)],
        out_specs=pl.BlockSpec(memory_space=pltpu.VMEM),
        scratch_shapes=[
            pltpu.VMEM((rows, width, width), jnp.bfloat16),
            pltpu.VMEM((4, rows // 2 * width, LANES), jnp.bfloat16),
            pltpu.SemaphoreType.DMA((4, PARTS)),
            pltpu.SemaphoreType.DMA((4, PARTS)),
        ],
        compiler_params=pltpu.CompilerParams(
            collective_id=0, has_side_effects=True, vmem_limit_bytes=24 * 2**20
        ),
        name="gather_prolong",
    )(prolong)


def turned_dot(left, right):
    return lax.dot_general(left, right, (((1,), (1,)), ((), ())), preferred_element_type=jnp.float32)


def product_kernel(col_ref, slot_ref, agg_ref, tile_ref, own_ref, blk_ref, out_ref, acc, product, term, back):
    step = pl.program_id(0)
    width = own_ref.shape[1]
    neighbours = blk_ref.shape[1]

    @pl.when(step == 0)
    def _():
        @pl.loop(0, acc.shape[0] // 384)
        def _(at):
            acc[pl.ds(at * 384, 384), :] = jnp.zeros((384, width), jnp.float32)

        product[...] = jnp.zeros_like(product)
        term[...] = jnp.zeros_like(term)

    last = own_ref.shape[0] - 1

    def add_term(i, k):
        base = pl.multiple_of((slot_ref[k, i] * CR_SLAB + agg_ref[i]) * width, width)
        acc[pl.ds(base, width), :] += term[pl.ds(k * width, width), :]

    def second(i, first, count):
        rows = pl.ds(first * width, count * width)
        term[rows, :] = jnp.dot(product[rows, :], own_ref[i], preferred_element_type=jnp.float32)

    @pl.loop(0, ROWS_STEP)
    def _(r):
        i = step * ROWS_STEP + r
        before, earlier = jnp.maximum(i - 1, 0), jnp.maximum(i - 2, 0)
        for first in range(0, neighbours, CHUNK):
            for k in range(first, first + CHUNK):
                add_term(earlier, k)
            second(before, first, CHUNK)
            for k in range(first, first + CHUNK):
                value = turned_dot(tile_ref[col_ref[k, i], :, :width], blk_ref[r, k])
                product[pl.ds(k * width, width), :] = value.astype(jnp.bfloat16)

    @pl.when(step == pl.num_programs(0) - 1)
    def _():
        for first in range(0, neighbours, CHUNK):
            for k in range(first, first + CHUNK):
                add_term(last - 1, k)
            second(last, first, CHUNK)
        for k in range(neighbours):
            add_term(last, k)

        lane = lax.broadcasted_iota(jnp.int32, (16, LANES), 1)
        same = placement(width, 0, 0)[:, :width]

        @pl.loop(0, GROUP // 16)
        def _(s):
            for t in range(16):
                sums = [
                    acc[pl.ds(pl.multiple_of((GROUP * q + 16 * s + t) * width, width), width), :].astype(jnp.bfloat16)
                    for q in range(GROUPS)
                ]
                value = turned_dot(same, jnp.concatenate(sums, axis=0))
                back[0, pl.ds(t * width, width), :] = value[:, :LANES]
                back[1, pl.ds(t * width, width), :GROUPS * width - LANES] = value[:, LANES:]

            rows = pl.ds(pl.multiple_of(16 * s, 16), 16)

            @pl.loop(0, 8)
            def _(d):
                for pair in range(3):
                    at = 6 * d + 2 * pair
                    low, high, low_next, high_next = (
                        back[j, pl.ds(at + r, 16, stride=width), :] for r in range(2) for j in range(2)
                    )
                    low_next, high_next = pltpu.roll(low_next, 64, 1), pltpu.roll(high_next, 64, 1)
                    parts = (low, jnp.where(lane < 64, high, low_next), jnp.where(lane < 64, low_next, high_next))
                    for j, part in enumerate(parts):
                        begin = (3 * pair + j) * LANES
                        out_ref[d, rows, begin:begin + LANES] = part.astype(jnp.bfloat16)


def products(tile, prolong, blocks, columns, aggregate, slots):
    rows, neighbours, width = blocks.shape[0], blocks.shape[1], blocks.shape[2]
    smem = pl.BlockSpec(memory_space=pltpu.SMEM)
    vmem = pl.BlockSpec(memory_space=pltpu.VMEM)
    flops = rows * neighbours * width**3 * 4
    return pl.pallas_call(
        product_kernel,
        grid=(rows // ROWS_STEP,),
        out_shape=jax.ShapeDtypeStruct((8, GROUP, 9 * LANES), jnp.bfloat16),
        in_specs=[
            smem,
            smem,
            smem,
            vmem,
            vmem,
            pl.BlockSpec((ROWS_STEP, neighbours, width, width), lambda g: (g, 0, 0, 0)),
        ],
        out_specs=vmem,
        scratch_shapes=[
            pltpu.VMEM((GROUPS * GROUP * width, width), jnp.float32),
            pltpu.VMEM((neighbours * width, width), jnp.bfloat16),
            pltpu.VMEM((neighbours * width, width), jnp.float32),
            pltpu.VMEM((2, 16 * width, LANES), jnp.float32),
        ],
        compiler_params=pltpu.CompilerParams(vmem_limit_bytes=40 * 2**20),
        cost_estimate=pl.CostEstimate(flops=flops, bytes_accessed=20 * 2**20, transcendentals=0),
        name="triple_products",
    )(columns.T, slots.T, aggregate, tile, prolong, blocks)


def scatter_kernel(x_ref, out_ref, ybuf, zsend, zbuf, own, ysend_sem, yrecv_sem, zsend_sem, zrecv_sem):
    me = lax.axis_index("col")
    y, z = me % 2, me // 2
    partner = z * 2 + 1 - y
    offsets = (2, 1, 3, 0)
    targets = [(z + offset) % 4 for offset in offsets]

    barrier = pltpu.get_barrier_semaphore()
    for peer in [partner] + [t * 2 + y for t in targets[:3]]:
        pl.semaphore_signal(barrier, inc=1, device_id={"col": peer}, device_id_type=MESH)
    pl.semaphore_wait(barrier, 4)

    ycopies, zcopies = {}, {}
    for s in range(4):
        for h, (begin, size) in enumerate(HALVES):
            copy = pltpu.make_async_remote_copy(
                src_ref=x_ref.at[targets[s] * 2 + 1 - y, pl.ds(begin, size)],
                dst_ref=ybuf.at[s, pl.ds(begin, size)],
                send_sem=ysend_sem.at[s, h],
                recv_sem=yrecv_sem.at[s, h],
                device_id={"col": partner},
                device_id_type=MESH,
            )
            copy.start()
            ycopies[s, h] = copy

    for s in range(4):
        for h, (begin, size) in enumerate(HALVES):
            ycopies[s, h].wait_recv()

            @pl.loop(begin // 16, (begin + size) // 16)
            def _(at):
                rows = pl.ds(pl.multiple_of(at * 16, 16), 16)
                total = x_ref[targets[s] * 2 + y, rows, :].astype(jnp.float32) + ybuf[s, rows, :].astype(jnp.float32)
                if s < 3:
                    zsend[s, rows, :] = total.astype(jnp.bfloat16)
                else:
                    own[rows, :] = total

            if s < 3:
                copy = pltpu.make_async_remote_copy(
                    src_ref=zsend.at[s, pl.ds(begin, size)],
                    dst_ref=zbuf.at[s, pl.ds(begin, size)],
                    send_sem=zsend_sem.at[s, h],
                    recv_sem=zrecv_sem.at[s, h],
                    device_id={"col": targets[s] * 2 + y},
                    device_id_type=MESH,
                )
                copy.start()
                zcopies[s, h] = copy

    for copy in zcopies.values():
        copy.wait_recv()

    lane = lax.broadcasted_iota(jnp.int32, (16, LANES), 1)

    def unpack(at, groups):
        rows = pl.ds(pl.multiple_of(at * 16, 16), 16)
        total = own[rows, :]
        for s in range(3):
            total = total + zbuf[s, rows, :].astype(jnp.float32)
        tiles = [total[:, j * LANES:(j + 1) * LANES] for j in range(9)]
        for q in range(groups):
            parts = [None] * 3
            for r in range(6):
                source, dest = 192 * r + 48 * q, 48 * r
                shift = (dest - source) % LANES
                for j in range(source // LANES, (source + 47) // LANES + 1):
                    begin = max(source, LANES * j) - source + dest
                    end = min(source + 48, LANES * (j + 1)) - source + dest
                    piece = pltpu.roll(tiles[j], shift, 1) if shift else tiles[j]
                    for m in range(begin // LANES, (end - 1) // LANES + 1):
                        low = max(begin - LANES * m, 0)
                        parts[m] = jnp.where(lane < low, parts[m], piece) if low else piece
            target = pl.ds(pl.multiple_of(GROUP * q + at * 16, 16), 16)
            for m in range(2):
                out_ref[target, m * LANES:(m + 1) * LANES] = parts[m]
            out_ref[target, 256:288] = parts[2][:, :32]

    @pl.loop(0, 6)
    def _(at):
        unpack(at, 4)

    unpack(6, 3)

    for copy in list(ycopies.values()) + list(zcopies.values()):
        copy.wait_send()


def scatter_cols(packed):
    half = len(HALVES)
    return pl.pallas_call(
        scatter_kernel,
        out_shape=jax.ShapeDtypeStruct((KC * CR_SLAB, 288), jnp.float32),
        in_specs=[pl.BlockSpec(memory_space=pltpu.VMEM)],
        out_specs=pl.BlockSpec(memory_space=pltpu.VMEM),
        scratch_shapes=[
            pltpu.VMEM((4, GROUP, 9 * LANES), jnp.bfloat16),
            pltpu.VMEM((3, GROUP, 9 * LANES), jnp.bfloat16),
            pltpu.VMEM((3, GROUP, 9 * LANES), jnp.bfloat16),
            pltpu.VMEM((GROUP, 9 * LANES), jnp.float32),
            pltpu.SemaphoreType.DMA((4, half)),
            pltpu.SemaphoreType.DMA((4, half)),
            pltpu.SemaphoreType.DMA((3, half)),
            pltpu.SemaphoreType.DMA((3, half)),
        ],
        compiler_params=pltpu.CompilerParams(
            collective_id=1, has_side_effects=True, vmem_limit_bytes=24 * 2**20
        ),
        name="scatter_cols",
    )(packed)


def shards(n_row, blocks, prolong, columns, aggregate, slots):
    tile = gather_rows(prolong, n_row)
    packed = products(tile, prolong, blocks, columns, aggregate, slots)
    result = scatter_cols(packed)
    return result.reshape(KC, CR_SLAB, 288).transpose(1, 0, 2)


def shards_any(blocks, prolong, columns, aggregate, slots):
    width = blocks.shape[2]
    tile = lax.all_gather(prolong, "row", axis=0, tiled=True)
    picked = jnp.take(tile, columns, axis=0)
    product = jnp.einsum(
        "rkab,rkbc->rkac", blocks, picked, preferred_element_type=jnp.float32
    ).astype(jnp.bfloat16)
    term = jnp.einsum("rba,rkbc->rkac", prolong, product, preferred_element_type=jnp.float32)
    target = (aggregate[:, None] * KC + slots).reshape(-1)
    partial_value = jax.ops.segment_sum(
        term.reshape(-1, width * width), target, num_segments=CR_SLAB * KC
    )
    partial_value = partial_value.reshape(CR_SLAB, KC, width * width)
    summed = lax.psum(partial_value, "col")
    share = width * width // lax.axis_size("col")
    return lax.dynamic_slice_in_dim(summed, lax.axis_index("col") * share, share, 2)


def solution(mesh):
    n_row, n_col = mesh.shape["row"], mesh.shape["col"]
    body = functools.partial(shards, n_row) if (n_row, n_col) == (4, 8) else shards_any
    return jax.shard_map(
        body,
        mesh=mesh,
        in_specs=(
            P(("row", "col"), None, None, None),
            P(("row", "col"), None, None),
            P(("row", "col"), None),
            P(("row", "col")),
            P(("row", "col"), None),
        ),
        out_specs=P("row", None, "col"),
        check_vma=False,
    )
```

```python
import functools

import jax
import jax.numpy as jnp
from jax import lax
from jax.experimental import pallas as pl
from jax.experimental.pallas import tpu as pltpu
from jax.sharding import PartitionSpec as P

KC = 27
CR_SLAB = 16
MESH = pl.DeviceIdType.MESH
LANES = 128
GROUPS = 4
GROUP = 112
ROWS_STEP = 4
PARTS = 3
HALVES = ((0, 32), (32, 32), (64, 32), (96, 16))


def placement(rows, source, dest):
    row = lax.broadcasted_iota(jnp.int32, (rows, LANES), 0)
    lane = lax.broadcasted_iota(jnp.int32, (rows, LANES), 1)
    keep = (row - source == lane - dest) & (row >= source) & (row < source + 48)
    return jnp.where(keep, 1.0, 0.0).astype(jnp.bfloat16)


def move(value, matrix):
    return jnp.dot(value, matrix, preferred_element_type=jnp.float32).astype(jnp.bfloat16)


def gather_kernel(p_ref, out_ref, packed, send_sem, recv_sem):
    rows, width = p_ref.shape[0], p_ref.shape[1]
    half = rows // 2
    me = lax.axis_index("row")
    core, x = me % 2, me // 2
    other = x * 2 + 1 - core
    across = (1 - x) * 2 + core
    diagonal = (1 - x) * 2 + 1 - core

    barrier = pltpu.get_barrier_semaphore()
    for peer in (other, across):
        pl.semaphore_signal(barrier, inc=1, device_id={"row": peer}, device_id_type=MESH)

    low = p_ref[:half].reshape(half * width, width)
    high = p_ref[half:].reshape(half * width, width)
    first, second = placement(width, 0, 0), placement(width, 0, 48)
    both = jnp.dot(low, first, preferred_element_type=jnp.float32) + jnp.dot(
        high, second, preferred_element_type=jnp.float32
    )
    packed[0] = both.astype(jnp.bfloat16)
    pl.semaphore_wait(barrier, 2)

    step = half * width // PARTS
    blocks = half // PARTS

    def send(source, dest, part, peer):
        copy = pltpu.make_async_remote_copy(
            src_ref=packed.at[source, pl.ds(part * step, step)],
            dst_ref=packed.at[dest, pl.ds(part * step, step)],
            send_sem=send_sem.at[dest, part],
            recv_sem=recv_sem.at[dest, part],
            device_id={"row": peer},
            device_id_type=MESH,
        )
        copy.start()
        return copy

    def unpack(slot, part, owner):
        value = packed[slot, pl.ds(part * step, step), :]
        for side in range(2):
            at = owner * rows + half * side + part * blocks
            piece = move(value, placement(LANES, 48 * side, 0))
            out_ref[pl.ds(at, blocks)] = piece.reshape(blocks, width, LANES)

    far = [send(0, 2, part, across) for part in range(PARTS)]
    near = [send(0, 1, part, other) for part in range(PARTS)]
    for part in range(PARTS):
        unpack(0, part, me)
    for part in range(PARTS):
        near[part].wait_recv()
        unpack(1, part, other)
    relay = []
    for part in range(PARTS):
        far[part].wait_recv()
        relay.append(send(2, 3, part, other))
        unpack(2, part, across)
    for part in range(PARTS):
        relay[part].wait_recv()
        unpack(3, part, diagonal)
    for copy in far + near + relay:
        copy.wait_send()


def gather_rows(prolong, n_row):
    rows, width = prolong.shape[0], prolong.shape[1]
    return pl.pallas_call(
        gather_kernel,
        out_shape=jax.ShapeDtypeStruct((n_row * rows, width, LANES), jnp.bfloat16),
        in_specs=[pl.BlockSpec(memory_space=pltpu.VMEM)],
        out_specs=pl.BlockSpec(memory_space=pltpu.VMEM),
        scratch_shapes=[
            pltpu.VMEM((4, rows // 2 * width, LANES), jnp.bfloat16),
            pltpu.SemaphoreType.DMA((4, PARTS)),
            pltpu.SemaphoreType.DMA((4, PARTS)),
        ],
        compiler_params=pltpu.CompilerParams(
            collective_id=0, has_side_effects=True, vmem_limit_bytes=24 * 2**20
        ),
        name="gather_prolong",
    )(prolong)


def product_kernel(col_ref, slot_ref, agg_ref, tile_ref, own_ref, blk_ref, out_ref, acc, product, term, turned):
    step = pl.program_id(0)
    width = own_ref.shape[1]
    neighbours = blk_ref.shape[1]

    @pl.when(step == 0)
    def _():
        @pl.loop(0, acc.shape[0] // 384)
        def _(at):
            acc[pl.ds(at * 384, 384), :] = jnp.zeros((384, LANES), jnp.float32)

        product[...] = jnp.zeros_like(product)
        term[...] = jnp.zeros_like(term)
        turned[...] = jnp.zeros_like(turned)

    last = own_ref.shape[0] - 1

    def add_terms(i, first):
        group = range(first, first + 3)
        slot = [slot_ref[k, i] for k in group]
        rows = [pl.ds(pl.multiple_of((n * CR_SLAB + agg_ref[i]) * width, width), width) for n in slot]
        old = [acc[at, :] for at in rows]
        terms = [term[k] for k in group]
        sums = list(terms)
        for later in range(1, 3):
            for earlier in range(later):
                sums[later] += jnp.where(slot[earlier] == slot[later], terms[earlier], 0.0)
        for at in range(3):
            acc[rows[at], :] = old[at] + sums[at]

    def second(k):
        term[k] = jnp.dot(turned[...], product[k], preferred_element_type=jnp.float32)

    @pl.loop(0, ROWS_STEP)
    def _(r):
        i = step * ROWS_STEP + r
        before = jnp.maximum(i - 2, 0)
        for first in range(0, neighbours, 3):
            add_terms(before, first)
            for k in range(first, first + 3):
                second(k)
            for k in range(first, first + 3):
                product[k] = jnp.dot(
                    blk_ref[r, k], tile_ref[col_ref[k, i]], preferred_element_type=jnp.float32
                ).astype(jnp.bfloat16)
        turned[...] = own_ref[i].astype(jnp.float32).T.astype(jnp.bfloat16)

    @pl.when(step == pl.num_programs(0) - 1)
    def _():
        for first in range(0, neighbours, 3):
            add_terms(last - 1, first)
            for k in range(first, first + 3):
                second(k)
        for first in range(0, neighbours, 3):
            add_terms(last, first)

    @pl.when(step == pl.num_programs(0) - 1)
    def _():
        lane = lax.broadcasted_iota(jnp.int32, (16, LANES), 1)

        @pl.loop(0, 8 * (GROUP // 16))
        def _(at):
            d, s = at // (GROUP // 16), at % (GROUP // 16)
            sums = [None] * 9
            for q in range(GROUPS):
                for r in range(6):
                    start = (GROUP * q + 16 * s) * width + 6 * d + r
                    offset = (q * 6 + r) * 48
                    j, shift = offset // LANES, offset % LANES
                    value = acc[pl.ds(start, 16, stride=width), :]
                    if shift:
                        value = pltpu.roll(value, shift, 1)
                    over = shift + 48 - LANES
                    if over > 0:
                        spill = jnp.where(lane < over, value, 0.0)
                        value = jnp.where(lane < over, 0.0, value)
                        sums[j + 1] = spill
                    sums[j] = value if sums[j] is None else sums[j] + value
            for j in range(9):
                out_ref[d, pl.ds(pl.multiple_of(16 * s, 16), 16), j * LANES:(j + 1) * LANES] = sums[j].astype(jnp.bfloat16)


def products(tile, prolong, blocks, columns, aggregate, slots):
    rows, neighbours, width = blocks.shape[0], blocks.shape[1], blocks.shape[2]
    smem = pl.BlockSpec(memory_space=pltpu.SMEM)
    vmem = pl.BlockSpec(memory_space=pltpu.VMEM)
    flops = rows * neighbours * width**3 * 4
    return pl.pallas_call(
        product_kernel,
        grid=(rows // ROWS_STEP,),
        out_shape=jax.ShapeDtypeStruct((8, GROUP, 9 * LANES), jnp.bfloat16),
        in_specs=[
            smem,
            smem,
            smem,
            vmem,
            vmem,
            pl.BlockSpec((ROWS_STEP, neighbours, width, width), lambda g: (g, 0, 0, 0)),
        ],
        out_specs=vmem,
        scratch_shapes=[
            pltpu.VMEM((GROUPS * GROUP * width, LANES), jnp.float32),
            pltpu.VMEM((neighbours, width, LANES), jnp.bfloat16),
            pltpu.VMEM((neighbours, width, LANES), jnp.float32),
            pltpu.VMEM((width, width), jnp.bfloat16),
        ],
        compiler_params=pltpu.CompilerParams(vmem_limit_bytes=40 * 2**20),
        cost_estimate=pl.CostEstimate(flops=flops, bytes_accessed=20 * 2**20, transcendentals=0),
        name="triple_products",
    )(columns.T, slots.T, aggregate, tile, prolong, blocks)


def scatter_kernel(x_ref, out_ref, ybuf, zsend, zbuf, own, ysend_sem, yrecv_sem, zsend_sem, zrecv_sem):
    me = lax.axis_index("col")
    y, z = me % 2, me // 2
    partner = z * 2 + 1 - y
    offsets = (2, 1, 3, 0)
    targets = [(z + offset) % 4 for offset in offsets]

    barrier = pltpu.get_barrier_semaphore()
    for peer in [partner] + [t * 2 + y for t in targets[:3]]:
        pl.semaphore_signal(barrier, inc=1, device_id={"col": peer}, device_id_type=MESH)
    pl.semaphore_wait(barrier, 4)

    ycopies, zcopies = {}, {}
    for s in range(4):
        for h, (begin, size) in enumerate(HALVES):
            copy = pltpu.make_async_remote_copy(
                src_ref=x_ref.at[targets[s] * 2 + 1 - y, pl.ds(begin, size)],
                dst_ref=ybuf.at[s, pl.ds(begin, size)],
                send_sem=ysend_sem.at[s, h],
                recv_sem=yrecv_sem.at[s, h],
                device_id={"col": partner},
                device_id_type=MESH,
            )
            copy.start()
            ycopies[s, h] = copy

    for s in range(4):
        for h, (begin, size) in enumerate(HALVES):
            ycopies[s, h].wait_recv()

            @pl.loop(begin // 16, (begin + size) // 16)
            def _(at):
                rows = pl.ds(pl.multiple_of(at * 16, 16), 16)
                total = x_ref[targets[s] * 2 + y, rows, :].astype(jnp.float32) + ybuf[s, rows, :].astype(jnp.float32)
                if s < 3:
                    zsend[s, rows, :] = total.astype(jnp.bfloat16)
                else:
                    own[rows, :] = total

            if s < 3:
                copy = pltpu.make_async_remote_copy(
                    src_ref=zsend.at[s, pl.ds(begin, size)],
                    dst_ref=zbuf.at[s, pl.ds(begin, size)],
                    send_sem=zsend_sem.at[s, h],
                    recv_sem=zrecv_sem.at[s, h],
                    device_id={"col": targets[s] * 2 + y},
                    device_id_type=MESH,
                )
                copy.start()
                zcopies[s, h] = copy

    lane = lax.broadcasted_iota(jnp.int32, (16, LANES), 1)

    def unpack(at, groups):
        rows = pl.ds(at * 16, 16)
        total = own[rows, :]
        for s in range(3):
            total = total + zbuf[s, rows, :].astype(jnp.float32)
        for q in range(groups):
            j, shift = 288 * q // LANES, 288 * q % LANES
            turned = [total[:, (j + m) * LANES:(j + m + 1) * LANES] for m in range(3)]
            if shift:
                turned = [pltpu.roll(piece, LANES - shift, 1) for piece in turned]
            target = pl.ds(GROUP * q + at * 16, 16)
            for m in range(2):
                piece = turned[m]
                if shift:
                    piece = jnp.where(lane < LANES - shift, piece, turned[m + 1])
                out_ref[target, m * LANES:(m + 1) * LANES] = piece
            out_ref[target, 256:288] = turned[2][:, :32]

    for h, (begin, size) in enumerate(HALVES):
        for s in range(3):
            zcopies[s, h].wait_recv()
        for at in range(begin // 16, (begin + size) // 16):
            unpack(at, 4 if at < 6 else 3)

    for copy in list(ycopies.values()) + list(zcopies.values()):
        copy.wait_send()


def scatter_cols(packed):
    half = len(HALVES)
    return pl.pallas_call(
        scatter_kernel,
        out_shape=jax.ShapeDtypeStruct((KC * CR_SLAB, 288), jnp.float32),
        in_specs=[pl.BlockSpec(memory_space=pltpu.VMEM)],
        out_specs=pl.BlockSpec(memory_space=pltpu.VMEM),
        scratch_shapes=[
            pltpu.VMEM((4, GROUP, 9 * LANES), jnp.bfloat16),
            pltpu.VMEM((3, GROUP, 9 * LANES), jnp.bfloat16),
            pltpu.VMEM((3, GROUP, 9 * LANES), jnp.bfloat16),
            pltpu.VMEM((GROUP, 9 * LANES), jnp.float32),
            pltpu.SemaphoreType.DMA((4, half)),
            pltpu.SemaphoreType.DMA((4, half)),
            pltpu.SemaphoreType.DMA((3, half)),
            pltpu.SemaphoreType.DMA((3, half)),
        ],
        compiler_params=pltpu.CompilerParams(
            collective_id=1, has_side_effects=True, vmem_limit_bytes=24 * 2**20
        ),
        name="scatter_cols",
    )(packed)


def shards(n_row, blocks, prolong, columns, aggregate, slots):
    tile = gather_rows(prolong, n_row)
    packed = products(tile, prolong, blocks, columns, aggregate, slots)
    result = scatter_cols(packed)
    return result.reshape(KC, CR_SLAB, 288).transpose(1, 0, 2)


def shards_any(blocks, prolong, columns, aggregate, slots):
    width = blocks.shape[2]
    tile = lax.all_gather(prolong, "row", axis=0, tiled=True)
    picked = jnp.take(tile, columns, axis=0)
    product = jnp.einsum(
        "rkab,rkbc->rkac", blocks, picked, preferred_element_type=jnp.float32
    ).astype(jnp.bfloat16)
    term = jnp.einsum("rba,rkbc->rkac", prolong, product, preferred_element_type=jnp.float32)
    target = (aggregate[:, None] * KC + slots).reshape(-1)
    partial_value = jax.ops.segment_sum(
        term.reshape(-1, width * width), target, num_segments=CR_SLAB * KC
    )
    partial_value = partial_value.reshape(CR_SLAB, KC, width * width)
    summed = lax.psum(partial_value, "col")
    share = width * width // lax.axis_size("col")
    return lax.dynamic_slice_in_dim(summed, lax.axis_index("col") * share, share, 2)


def solution(mesh):
    n_row, n_col = mesh.shape["row"], mesh.shape["col"]
    body = functools.partial(shards, n_row) if (n_row, n_col) == (4, 8) else shards_any
    return jax.shard_map(
        body,
        mesh=mesh,
        in_specs=(
            P(("row", "col"), None, None, None),
            P(("row", "col"), None, None),
            P(("row", "col"), None),
            P(("row", "col")),
            P(("row", "col"), None),
        ),
        out_specs=P("row", None, "col"),
        check_vma=False,
    )
```

```python
import functools

import jax
import jax.numpy as jnp
from jax import lax
from jax.experimental import pallas as pl
from jax.experimental.pallas import tpu as pltpu
from jax.sharding import PartitionSpec as P

KC = 27
CR_SLAB = 16
MESH = pl.DeviceIdType.MESH
LANES = 128
GROUPS = 4
GROUP = 112
ROWS_STEP = 4
PARTS = 3
HALVES = ((0, 32), (32, 32), (64, 32), (96, 16))


def placement(rows, source, dest):
    row = lax.broadcasted_iota(jnp.int32, (rows, LANES), 0)
    lane = lax.broadcasted_iota(jnp.int32, (rows, LANES), 1)
    keep = (row - source == lane - dest) & (row >= source) & (row < source + 48)
    return jnp.where(keep, 1.0, 0.0).astype(jnp.bfloat16)


def move(value, matrix):
    return jnp.dot(value, matrix, preferred_element_type=jnp.float32).astype(jnp.bfloat16)


def gather_kernel(p_ref, out_ref, packed, send_sem, recv_sem):
    rows, width = p_ref.shape[0], p_ref.shape[1]
    half = rows // 2
    me = lax.axis_index("row")
    core, x = me % 2, me // 2
    other = x * 2 + 1 - core
    across = (1 - x) * 2 + core
    diagonal = (1 - x) * 2 + 1 - core

    barrier = pltpu.get_barrier_semaphore()
    for peer in (other, across):
        pl.semaphore_signal(barrier, inc=1, device_id={"row": peer}, device_id_type=MESH)

    low = p_ref[:half].reshape(half * width, width)
    high = p_ref[half:].reshape(half * width, width)
    first, second = placement(width, 0, 0), placement(width, 0, 48)
    both = jnp.dot(low, first, preferred_element_type=jnp.float32) + jnp.dot(
        high, second, preferred_element_type=jnp.float32
    )
    packed[0] = both.astype(jnp.bfloat16)
    pl.semaphore_wait(barrier, 2)

    step = half * width // PARTS
    blocks = half // PARTS

    def send(source, dest, part, peer):
        copy = pltpu.make_async_remote_copy(
            src_ref=packed.at[source, pl.ds(part * step, step)],
            dst_ref=packed.at[dest, pl.ds(part * step, step)],
            send_sem=send_sem.at[dest, part],
            recv_sem=recv_sem.at[dest, part],
            device_id={"row": peer},
            device_id_type=MESH,
        )
        copy.start()
        return copy

    def unpack(slot, part, owner):
        value = packed[slot, pl.ds(part * step, step), :]
        for side in range(2):
            at = owner * rows + half * side + part * blocks
            piece = move(value, placement(LANES, 48 * side, 0))
            out_ref[pl.ds(at, blocks)] = piece.reshape(blocks, width, LANES)

    far = [send(0, 2, part, across) for part in range(PARTS)]
    near = [send(0, 1, part, other) for part in range(PARTS)]
    for part in range(PARTS):
        unpack(0, part, me)
    for part in range(PARTS):
        near[part].wait_recv()
        unpack(1, part, other)
    relay = []
    for part in range(PARTS):
        far[part].wait_recv()
        relay.append(send(2, 3, part, other))
        unpack(2, part, across)
    for part in range(PARTS):
        relay[part].wait_recv()
        unpack(3, part, diagonal)
    for copy in far + near + relay:
        copy.wait_send()


def gather_rows(prolong, n_row):
    rows, width = prolong.shape[0], prolong.shape[1]
    return pl.pallas_call(
        gather_kernel,
        out_shape=jax.ShapeDtypeStruct((n_row * rows, width, LANES), jnp.bfloat16),
        in_specs=[pl.BlockSpec(memory_space=pltpu.VMEM)],
        out_specs=pl.BlockSpec(memory_space=pltpu.VMEM),
        scratch_shapes=[
            pltpu.VMEM((4, rows // 2 * width, LANES), jnp.bfloat16),
            pltpu.SemaphoreType.DMA((4, PARTS)),
            pltpu.SemaphoreType.DMA((4, PARTS)),
        ],
        compiler_params=pltpu.CompilerParams(
            collective_id=0, has_side_effects=True, vmem_limit_bytes=24 * 2**20
        ),
        name="gather_prolong",
    )(prolong)


def product_kernel(col_ref, slot_ref, agg_ref, tile_ref, own_ref, blk_ref, acc, product, term, turned):
    step = pl.program_id(0)
    width = own_ref.shape[1]
    neighbours = blk_ref.shape[1]

    @pl.when(step == 0)
    def _():
        @pl.loop(0, acc.shape[0] // 384)
        def _(at):
            acc[pl.ds(at * 384, 384), :] = jnp.zeros((384, LANES), jnp.float32)

        product[...] = jnp.zeros_like(product)
        term[...] = jnp.zeros_like(term)
        turned[...] = jnp.zeros_like(turned)

    last = own_ref.shape[0] - 1

    def add_terms(i, first):
        group = range(first, first + 3)
        slot = [slot_ref[k, i] for k in group]
        rows = [pl.ds(pl.multiple_of((n * CR_SLAB + agg_ref[i]) * width, width), width) for n in slot]
        old = [acc[at, :] for at in rows]
        terms = [term[k] for k in group]
        sums = list(terms)
        for later in range(1, 3):
            for earlier in range(later):
                sums[later] += jnp.where(slot[earlier] == slot[later], terms[earlier], 0.0)
        for at in range(3):
            acc[rows[at], :] = old[at] + sums[at]

    def second(k):
        term[k] = jnp.dot(turned[...], product[k], preferred_element_type=jnp.float32)

    @pl.loop(0, ROWS_STEP)
    def _(r):
        i = step * ROWS_STEP + r
        before = jnp.maximum(i - 2, 0)
        for first in range(0, neighbours, 3):
            add_terms(before, first)
            for k in range(first, first + 3):
                second(k)
            for k in range(first, first + 3):
                product[k] = jnp.dot(
                    blk_ref[r, k], tile_ref[col_ref[k, i]], preferred_element_type=jnp.float32
                ).astype(jnp.bfloat16)
        turned[...] = own_ref[i].astype(jnp.float32).T.astype(jnp.bfloat16)

    @pl.when(step == pl.num_programs(0) - 1)
    def _():
        for first in range(0, neighbours, 3):
            add_terms(last - 1, first)
            for k in range(first, first + 3):
                second(k)
        for first in range(0, neighbours, 3):
            add_terms(last, first)


def products(tile, prolong, blocks, columns, aggregate, slots):
    rows, neighbours, width = blocks.shape[0], blocks.shape[1], blocks.shape[2]
    smem = pl.BlockSpec(memory_space=pltpu.SMEM)
    vmem = pl.BlockSpec(memory_space=pltpu.VMEM)
    flops = rows * neighbours * width**3 * 4
    return pl.pallas_call(
        product_kernel,
        grid=(rows // ROWS_STEP,),
        out_shape=jax.ShapeDtypeStruct((GROUPS * GROUP * width, LANES), jnp.float32),
        in_specs=[
            smem,
            smem,
            smem,
            vmem,
            vmem,
            pl.BlockSpec((ROWS_STEP, neighbours, width, width), lambda g: (g, 0, 0, 0)),
        ],
        out_specs=vmem,
        scratch_shapes=[
            pltpu.VMEM((neighbours, width, LANES), jnp.bfloat16),
            pltpu.VMEM((neighbours, width, LANES), jnp.float32),
            pltpu.VMEM((width, width), jnp.bfloat16),
        ],
        compiler_params=pltpu.CompilerParams(vmem_limit_bytes=40 * 2**20),
        cost_estimate=pl.CostEstimate(flops=flops, bytes_accessed=20 * 2**20, transcendentals=0),
        name="triple_products",
    )(columns.T, slots.T, aggregate, tile, prolong, blocks)


def pack_rows(acc, d, at):
    lane = lax.broadcasted_iota(jnp.int32, (16, LANES), 1)
    sums = [None] * 9
    for q in range(GROUPS):
        for r in range(6):
            start = (GROUP * q + 16 * at) * 48 + 6 * d + r
            offset = (q * 6 + r) * 48
            j, shift = offset // LANES, offset % LANES
            value = acc[pl.ds(start, 16, stride=48), :]
            if shift:
                value = pltpu.roll(value, shift, 1)
            sums[j] = jnp.where(lane < shift, sums[j], value) if shift else value
            if shift + 48 > LANES:
                sums[j + 1] = value
    return sums


def scatter_kernel(acc, out_ref, ysend, ybuf, zsend, zbuf, own, ysend_sem, yrecv_sem, zsend_sem, zrecv_sem):
    me = lax.axis_index("col")
    y, z = me % 2, me // 2
    partner = z * 2 + 1 - y
    offsets = (2, 1, 3, 0)
    targets = [(z + offset) % 4 for offset in offsets]

    barrier = pltpu.get_barrier_semaphore()
    for peer in [partner] + [t * 2 + y for t in targets[:3]]:
        pl.semaphore_signal(barrier, inc=1, device_id={"col": peer}, device_id_type=MESH)

    ycopies, zcopies = {}, {}
    for s in range(4):
        for h, (begin, size) in enumerate(HALVES):

            @pl.loop(begin // 16, (begin + size) // 16)
            def _(at):
                rows = pl.ds(pl.multiple_of(at * 16, 16), 16)
                for j, part in enumerate(pack_rows(acc, targets[s] * 2 + 1 - y, at)):
                    ysend[s, rows, j * LANES:(j + 1) * LANES] = part.astype(jnp.bfloat16)

            if s == 0 and h == 0:
                pl.semaphore_wait(barrier, 4)
            copy = pltpu.make_async_remote_copy(
                src_ref=ysend.at[s, pl.ds(begin, size)],
                dst_ref=ybuf.at[s, pl.ds(begin, size)],
                send_sem=ysend_sem.at[s, h],
                recv_sem=yrecv_sem.at[s, h],
                device_id={"col": partner},
                device_id_type=MESH,
            )
            copy.start()
            ycopies[s, h] = copy

    for s in range(4):
        for h, (begin, size) in enumerate(HALVES):
            ycopies[s, h].wait_recv()

            @pl.loop(begin // 16, (begin + size) // 16)
            def _(at):
                rows = pl.ds(pl.multiple_of(at * 16, 16), 16)
                for j, part in enumerate(pack_rows(acc, targets[s] * 2 + y, at)):
                    lanes = slice(j * LANES, (j + 1) * LANES)
                    total = part + ybuf[s, rows, lanes].astype(jnp.float32)
                    if s < 3:
                        zsend[s, rows, lanes] = total.astype(jnp.bfloat16)
                    else:
                        own[rows, lanes] = total

            if s < 3:
                copy = pltpu.make_async_remote_copy(
                    src_ref=zsend.at[s, pl.ds(begin, size)],
                    dst_ref=zbuf.at[s, pl.ds(begin, size)],
                    send_sem=zsend_sem.at[s, h],
                    recv_sem=zrecv_sem.at[s, h],
                    device_id={"col": targets[s] * 2 + y},
                    device_id_type=MESH,
                )
                copy.start()
                zcopies[s, h] = copy

    lane = lax.broadcasted_iota(jnp.int32, (16, LANES), 1)

    def unpack(at, groups):
        rows = pl.ds(at * 16, 16)
        total = own[rows, :]
        for s in range(3):
            total = total + zbuf[s, rows, :].astype(jnp.float32)
        for q in range(groups):
            j, shift = 288 * q // LANES, 288 * q % LANES
            turned = [total[:, (j + m) * LANES:(j + m + 1) * LANES] for m in range(3)]
            if shift:
                turned = [pltpu.roll(piece, LANES - shift, 1) for piece in turned]
            target = pl.ds(GROUP * q + at * 16, 16)
            for m in range(2):
                piece = turned[m]
                if shift:
                    piece = jnp.where(lane < LANES - shift, piece, turned[m + 1])
                out_ref[target, m * LANES:(m + 1) * LANES] = piece
            out_ref[target, 256:288] = turned[2][:, :32]

    for h, (begin, size) in enumerate(HALVES):
        for s in range(3):
            zcopies[s, h].wait_recv()
        for at in range(begin // 16, (begin + size) // 16):
            unpack(at, 4 if at < 6 else 3)

    for copy in list(ycopies.values()) + list(zcopies.values()):
        copy.wait_send()


def scatter_cols(packed):
    half = len(HALVES)
    return pl.pallas_call(
        scatter_kernel,
        out_shape=jax.ShapeDtypeStruct((KC * CR_SLAB, 288), jnp.float32),
        in_specs=[pl.BlockSpec(memory_space=pltpu.VMEM)],
        out_specs=pl.BlockSpec(memory_space=pltpu.VMEM),
        scratch_shapes=[
            pltpu.VMEM((4, GROUP, 9 * LANES), jnp.bfloat16),
            pltpu.VMEM((4, GROUP, 9 * LANES), jnp.bfloat16),
            pltpu.VMEM((3, GROUP, 9 * LANES), jnp.bfloat16),
            pltpu.VMEM((3, GROUP, 9 * LANES), jnp.bfloat16),
            pltpu.VMEM((GROUP, 9 * LANES), jnp.float32),
            pltpu.SemaphoreType.DMA((4, half)),
            pltpu.SemaphoreType.DMA((4, half)),
            pltpu.SemaphoreType.DMA((3, half)),
            pltpu.SemaphoreType.DMA((3, half)),
        ],
        compiler_params=pltpu.CompilerParams(
            collective_id=1, has_side_effects=True, vmem_limit_bytes=24 * 2**20
        ),
        name="scatter_cols",
    )(packed)


def shards(n_row, blocks, prolong, columns, aggregate, slots):
    tile = gather_rows(prolong, n_row)
    packed = products(tile, prolong, blocks, columns, aggregate, slots)
    result = scatter_cols(packed)
    return result.reshape(KC, CR_SLAB, 288).transpose(1, 0, 2)


def shards_any(blocks, prolong, columns, aggregate, slots):
    width = blocks.shape[2]
    tile = lax.all_gather(prolong, "row", axis=0, tiled=True)
    picked = jnp.take(tile, columns, axis=0)
    product = jnp.einsum(
        "rkab,rkbc->rkac", blocks, picked, preferred_element_type=jnp.float32
    ).astype(jnp.bfloat16)
    term = jnp.einsum("rba,rkbc->rkac", prolong, product, preferred_element_type=jnp.float32)
    target = (aggregate[:, None] * KC + slots).reshape(-1)
    partial_value = jax.ops.segment_sum(
        term.reshape(-1, width * width), target, num_segments=CR_SLAB * KC
    )
    partial_value = partial_value.reshape(CR_SLAB, KC, width * width)
    summed = lax.psum(partial_value, "col")
    share = width * width // lax.axis_size("col")
    return lax.dynamic_slice_in_dim(summed, lax.axis_index("col") * share, share, 2)


def solution(mesh):
    n_row, n_col = mesh.shape["row"], mesh.shape["col"]
    body = functools.partial(shards, n_row) if (n_row, n_col) == (4, 8) else shards_any
    return jax.shard_map(
        body,
        mesh=mesh,
        in_specs=(
            P(("row", "col"), None, None, None),
            P(("row", "col"), None, None),
            P(("row", "col"), None),
            P(("row", "col")),
            P(("row", "col"), None),
        ),
        out_specs=P("row", None, "col"),
        check_vma=False,
    )
```

```python
import functools

import jax
import jax.numpy as jnp
from jax import lax
from jax.experimental import pallas as pl
from jax.experimental.pallas import tpu as pltpu
from jax.sharding import PartitionSpec as P

KC = 27
CR_SLAB = 16
MESH = pl.DeviceIdType.MESH
LANES = 128
GROUPS = 4
GROUP = 112
ROWS_STEP = 8
PARTS = 3
HALVES = ((0, 32), (32, 32), (64, 32), (96, 16))


def placement(rows, source, dest):
    row = lax.broadcasted_iota(jnp.int32, (rows, LANES), 0)
    lane = lax.broadcasted_iota(jnp.int32, (rows, LANES), 1)
    keep = (row - source == lane - dest) & (row >= source) & (row < source + 48)
    return jnp.where(keep, 1.0, 0.0).astype(jnp.bfloat16)


def move(value, matrix):
    return jnp.dot(value, matrix, preferred_element_type=jnp.float32).astype(jnp.bfloat16)


def gather_kernel(p_ref, out_ref, packed, send_sem, recv_sem):
    rows, width = p_ref.shape[0], p_ref.shape[1]
    half = rows // 2
    me = lax.axis_index("row")
    core, x = me % 2, me // 2
    other = x * 2 + 1 - core
    across = (1 - x) * 2 + core
    diagonal = (1 - x) * 2 + 1 - core

    barrier = pltpu.get_barrier_semaphore()
    for peer in (other, across):
        pl.semaphore_signal(barrier, inc=1, device_id={"row": peer}, device_id_type=MESH)

    low = p_ref[:half].reshape(half * width, width)
    high = p_ref[half:].reshape(half * width, width)
    first, second = placement(width, 0, 0), placement(width, 0, 48)
    both = jnp.dot(low, first, preferred_element_type=jnp.float32) + jnp.dot(
        high, second, preferred_element_type=jnp.float32
    )
    packed[0] = both.astype(jnp.bfloat16)
    pl.semaphore_wait(barrier, 2)

    step = half * width // PARTS
    blocks = half // PARTS

    def send(source, dest, part, peer):
        copy = pltpu.make_async_remote_copy(
            src_ref=packed.at[source, pl.ds(part * step, step)],
            dst_ref=packed.at[dest, pl.ds(part * step, step)],
            send_sem=send_sem.at[dest, part],
            recv_sem=recv_sem.at[dest, part],
            device_id={"row": peer},
            device_id_type=MESH,
        )
        copy.start()
        return copy

    def unpack(slot, part, owner):
        value = packed[slot, pl.ds(part * step, step), :]
        for side in range(2):
            at = owner * rows + half * side + part * blocks
            piece = move(value, placement(LANES, 48 * side, 0))
            out_ref[pl.ds(at, blocks)] = piece.reshape(blocks, width, LANES)

    far = [send(0, 2, part, across) for part in range(PARTS)]
    near = [send(0, 1, part, other) for part in range(PARTS)]
    for part in range(PARTS):
        unpack(0, part, me)
    for part in range(PARTS):
        near[part].wait_recv()
        unpack(1, part, other)
    relay = []
    for part in range(PARTS):
        far[part].wait_recv()
        relay.append(send(2, 3, part, other))
        unpack(2, part, across)
    for part in range(PARTS):
        relay[part].wait_recv()
        unpack(3, part, diagonal)
    for copy in far + near + relay:
        copy.wait_send()


def gather_rows(prolong, n_row):
    rows, width = prolong.shape[0], prolong.shape[1]
    return pl.pallas_call(
        gather_kernel,
        out_shape=jax.ShapeDtypeStruct((n_row * rows, width, LANES), jnp.bfloat16),
        in_specs=[pl.BlockSpec(memory_space=pltpu.VMEM)],
        out_specs=pl.BlockSpec(memory_space=pltpu.VMEM),
        scratch_shapes=[
            pltpu.VMEM((4, rows // 2 * width, LANES), jnp.bfloat16),
            pltpu.SemaphoreType.DMA((4, PARTS)),
            pltpu.SemaphoreType.DMA((4, PARTS)),
        ],
        compiler_params=pltpu.CompilerParams(
            collective_id=0, has_side_effects=True, vmem_limit_bytes=24 * 2**20
        ),
        name="gather_prolong",
    )(prolong)


def product_kernel(col_ref, slot_ref, agg_ref, tile_ref, own_ref, blk_ref, acc, product, term, turned):
    step = pl.program_id(0)
    width = own_ref.shape[1]
    neighbours = blk_ref.shape[1]

    @pl.when(step == 0)
    def _():
        @pl.loop(0, acc.shape[0] // 384)
        def _(at):
            acc[pl.ds(at * 384, 384), :] = jnp.zeros((384, LANES), jnp.float32)

        product[...] = jnp.zeros_like(product)
        term[...] = jnp.zeros_like(term)
        turned[...] = jnp.zeros_like(turned)

    last = own_ref.shape[0] - 1

    def add_terms(i, first):
        group = range(first, first + 3)
        slot = [slot_ref[k, i] for k in group]
        rows = [pl.ds(pl.multiple_of((n * CR_SLAB + agg_ref[i]) * width, width), width) for n in slot]
        old = [acc[at, :] for at in rows]
        terms = [term[k] for k in group]
        sums = list(terms)
        for later in range(1, 3):
            for earlier in range(later):
                sums[later] += jnp.where(slot[earlier] == slot[later], terms[earlier], 0.0)
        for at in range(3):
            acc[rows[at], :] = old[at] + sums[at]

    def second(k):
        term[k] = jnp.dot(turned[...], product[k], preferred_element_type=jnp.float32)

    @pl.loop(0, ROWS_STEP)
    def _(r):
        i = step * ROWS_STEP + r
        before = jnp.maximum(i - 2, 0)
        for first in range(0, neighbours, 3):
            add_terms(before, first)
            for k in range(first, first + 3):
                second(k)
            for k in range(first, first + 3):
                product[k] = jnp.dot(
                    blk_ref[r, k], tile_ref[col_ref[k, i]], preferred_element_type=jnp.float32
                ).astype(jnp.bfloat16)
        turned[...] = own_ref[i].astype(jnp.float32).T.astype(jnp.bfloat16)

    @pl.when(step == pl.num_programs(0) - 1)
    def _():
        for first in range(0, neighbours, 3):
            add_terms(last - 1, first)
            for k in range(first, first + 3):
                second(k)
        for first in range(0, neighbours, 3):
            add_terms(last, first)


def products(tile, prolong, blocks, columns, aggregate, slots):
    rows, neighbours, width = blocks.shape[0], blocks.shape[1], blocks.shape[2]
    smem = pl.BlockSpec(memory_space=pltpu.SMEM)
    vmem = pl.BlockSpec(memory_space=pltpu.VMEM)
    flops = rows * neighbours * width**3 * 4
    return pl.pallas_call(
        product_kernel,
        grid=(rows // ROWS_STEP,),
        out_shape=jax.ShapeDtypeStruct((GROUPS * GROUP * width, LANES), jnp.float32),
        in_specs=[
            smem,
            smem,
            smem,
            vmem,
            vmem,
            pl.BlockSpec((ROWS_STEP, neighbours, width, width), lambda g: (g, 0, 0, 0)),
        ],
        out_specs=vmem,
        scratch_shapes=[
            pltpu.VMEM((neighbours, width, LANES), jnp.bfloat16),
            pltpu.VMEM((neighbours, width, LANES), jnp.float32),
            pltpu.VMEM((width, width), jnp.bfloat16),
        ],
        compiler_params=pltpu.CompilerParams(vmem_limit_bytes=40 * 2**20),
        cost_estimate=pl.CostEstimate(flops=flops, bytes_accessed=20 * 2**20, transcendentals=0),
        name="triple_products",
    )(columns.T, slots.T, aggregate, tile, prolong, blocks)


def pack_rows(acc, d, at):
    lane = lax.broadcasted_iota(jnp.int32, (16, LANES), 1)
    sums = [None] * 9
    for q in range(GROUPS):
        for r in range(6):
            start = (GROUP * q + 16 * at) * 48 + 6 * d + r
            offset = (q * 6 + r) * 48
            j, shift = offset // LANES, offset % LANES
            value = acc[pl.ds(start, 16, stride=48), :]
            if shift:
                value = pltpu.roll(value, shift, 1)
            sums[j] = jnp.where(lane < shift, sums[j], value) if shift else value
            if shift + 48 > LANES:
                sums[j + 1] = value
    return sums


def scatter_kernel(acc, out_ref, ysend, ybuf, zsend, zbuf, own, ysend_sem, yrecv_sem, zsend_sem, zrecv_sem):
    me = lax.axis_index("col")
    y, z = me % 2, me // 2
    partner = z * 2 + 1 - y
    offsets = (2, 1, 3, 0)
    targets = [(z + offset) % 4 for offset in offsets]

    barrier = pltpu.get_barrier_semaphore()
    for peer in [partner] + [t * 2 + y for t in targets[:3]]:
        pl.semaphore_signal(barrier, inc=1, device_id={"col": peer}, device_id_type=MESH)

    ycopies, zcopies = {}, {}
    for s in range(4):
        for h, (begin, size) in enumerate(HALVES):

            @pl.loop(begin // 16, (begin + size) // 16)
            def _(at):
                rows = pl.ds(pl.multiple_of(at * 16, 16), 16)
                for j, part in enumerate(pack_rows(acc, targets[s] * 2 + 1 - y, at)):
                    ysend[s, rows, j * LANES:(j + 1) * LANES] = part.astype(jnp.bfloat16)

            if s == 0 and h == 0:
                pl.semaphore_wait(barrier, 4)
            copy = pltpu.make_async_remote_copy(
                src_ref=ysend.at[s, pl.ds(begin, size)],
                dst_ref=ybuf.at[s, pl.ds(begin, size)],
                send_sem=ysend_sem.at[s, h],
                recv_sem=yrecv_sem.at[s, h],
                device_id={"col": partner},
                device_id_type=MESH,
            )
            copy.start()
            ycopies[s, h] = copy

    for s in range(4):
        for h, (begin, size) in enumerate(HALVES):
            ycopies[s, h].wait_recv()

            @pl.loop(begin // 16, (begin + size) // 16)
            def _(at):
                rows = pl.ds(pl.multiple_of(at * 16, 16), 16)
                for j, part in enumerate(pack_rows(acc, targets[s] * 2 + y, at)):
                    lanes = slice(j * LANES, (j + 1) * LANES)
                    total = part + ybuf[s, rows, lanes].astype(jnp.float32)
                    if s < 3:
                        zsend[s, rows, lanes] = total.astype(jnp.bfloat16)
                    else:
                        own[rows, lanes] = total

            if s < 3:
                copy = pltpu.make_async_remote_copy(
                    src_ref=zsend.at[s, pl.ds(begin, size)],
                    dst_ref=zbuf.at[s, pl.ds(begin, size)],
                    send_sem=zsend_sem.at[s, h],
                    recv_sem=zrecv_sem.at[s, h],
                    device_id={"col": targets[s] * 2 + y},
                    device_id_type=MESH,
                )
                copy.start()
                zcopies[s, h] = copy

    lane = lax.broadcasted_iota(jnp.int32, (16, LANES), 1)

    def unpack(at, groups):
        rows = pl.ds(at * 16, 16)
        total = own[rows, :]
        for s in range(3):
            total = total + zbuf[s, rows, :].astype(jnp.float32)
        for q in range(groups):
            j, shift = 288 * q // LANES, 288 * q % LANES
            turned = [total[:, (j + m) * LANES:(j + m + 1) * LANES] for m in range(3)]
            if shift:
                turned = [pltpu.roll(piece, LANES - shift, 1) for piece in turned]
            target = pl.ds(GROUP * q + at * 16, 16)
            for m in range(2):
                piece = turned[m]
                if shift:
                    piece = jnp.where(lane < LANES - shift, piece, turned[m + 1])
                out_ref[target, m * LANES:(m + 1) * LANES] = piece
            out_ref[target, 256:288] = turned[2][:, :32]

    for h, (begin, size) in enumerate(HALVES):
        for s in range(3):
            zcopies[s, h].wait_recv()
        for at in range(begin // 16, (begin + size) // 16):
            unpack(at, 4 if at < 6 else 3)

    for copy in list(ycopies.values()) + list(zcopies.values()):
        copy.wait_send()


def scatter_cols(packed):
    half = len(HALVES)
    return pl.pallas_call(
        scatter_kernel,
        out_shape=jax.ShapeDtypeStruct((KC * CR_SLAB, 288), jnp.float32),
        in_specs=[pl.BlockSpec(memory_space=pltpu.VMEM)],
        out_specs=pl.BlockSpec(memory_space=pltpu.VMEM),
        scratch_shapes=[
            pltpu.VMEM((4, GROUP, 9 * LANES), jnp.bfloat16),
            pltpu.VMEM((4, GROUP, 9 * LANES), jnp.bfloat16),
            pltpu.VMEM((3, GROUP, 9 * LANES), jnp.bfloat16),
            pltpu.VMEM((3, GROUP, 9 * LANES), jnp.bfloat16),
            pltpu.VMEM((GROUP, 9 * LANES), jnp.float32),
            pltpu.SemaphoreType.DMA((4, half)),
            pltpu.SemaphoreType.DMA((4, half)),
            pltpu.SemaphoreType.DMA((3, half)),
            pltpu.SemaphoreType.DMA((3, half)),
        ],
        compiler_params=pltpu.CompilerParams(
            collective_id=1, has_side_effects=True, vmem_limit_bytes=24 * 2**20
        ),
        name="scatter_cols",
    )(packed)


def shards(n_row, blocks, prolong, columns, aggregate, slots):
    tile = gather_rows(prolong, n_row)
    packed = products(tile, prolong, blocks, columns, aggregate, slots)
    result = scatter_cols(packed)
    return result.reshape(KC, CR_SLAB, 288).transpose(1, 0, 2)


def shards_any(blocks, prolong, columns, aggregate, slots):
    width = blocks.shape[2]
    tile = lax.all_gather(prolong, "row", axis=0, tiled=True)
    picked = jnp.take(tile, columns, axis=0)
    product = jnp.einsum(
        "rkab,rkbc->rkac", blocks, picked, preferred_element_type=jnp.float32
    ).astype(jnp.bfloat16)
    term = jnp.einsum("rba,rkbc->rkac", prolong, product, preferred_element_type=jnp.float32)
    target = (aggregate[:, None] * KC + slots).reshape(-1)
    partial_value = jax.ops.segment_sum(
        term.reshape(-1, width * width), target, num_segments=CR_SLAB * KC
    )
    partial_value = partial_value.reshape(CR_SLAB, KC, width * width)
    summed = lax.psum(partial_value, "col")
    share = width * width // lax.axis_size("col")
    return lax.dynamic_slice_in_dim(summed, lax.axis_index("col") * share, share, 2)


def solution(mesh):
    n_row, n_col = mesh.shape["row"], mesh.shape["col"]
    body = functools.partial(shards, n_row) if (n_row, n_col) == (4, 8) else shards_any
    return jax.shard_map(
        body,
        mesh=mesh,
        in_specs=(
            P(("row", "col"), None, None, None),
            P(("row", "col"), None, None),
            P(("row", "col"), None),
            P(("row", "col")),
            P(("row", "col"), None),
        ),
        out_specs=P("row", None, "col"),
        check_vma=False,
    )
```
